128 devices in a mesh: cut: 16 (over y, x), depth: 8 (over z, core).
Axes of the slice: x: 4, y: 4, z: 4, core: 2. Of those that a mesh axis runs over, the one named last changes fastest.
Arguments:
- initial_state: float32 [9, 256, 128, 128], P(None, 'cut', 'depth'), may hold values from -6 to 6
- density: float32 [256, 128, 128], P('cut', 'depth'), may hold values from 0.5 to 2
- yield_flags: int32 [256, 128], P('cut', 'depth'), may hold values 0 or 1
- yield_stress: float32 [256, 128], P('cut', 'depth'), may hold values from 0.5 to 4
- crossing_weights: bfloat16 [65536, 128, 128], P(('cut', 'depth')), may hold values from 0.0029907227 to 0.099609375
- new_owner: int32 [65536, 1], P(('cut', 'depth')), may hold values from 0 to 127; in each aligned block of 512 rows (0 to 511, 512 to 1023, ...) at most 6 rows name the same one
- new_slot: int32 [65536], P(('cut', 'depth')), may hold values from 0 to 255
Outputs:
- state_after: float32 [9, 256, 128, 128], P(None, 'cut', 'depth')
- new_integrals: float32 [32768, 9, 128], P(('cut', 'depth'))
The draws below stay inside these ranges and needn't reach their ends.
Inputs may be any that keep to these rules, and one draw needn't show every extreme that they name: `new_owner`: among the 512 pairs of one device, at most 6 name the same owner, a bound that some block reaches of them.
All inputs are finite; a program needn't handle non-finite values. No bound on the sum of `yield_flags` on one device may be relied on, other than what follows from the above.
Results may differ from the reference program's by a relative error of at most 0.003.
Values sent between devices are 32-bit elements; how exact they have to be, the bound alone decides.
No kernel may reach another device: no remote copies, remote signals or barrier semaphores. Data moves between devices by JAX's collectives and lax.ppermute only.
A program may use at most 128 MiB of HBM per device.

```python
import math
import jax
import jax.numpy as jnp
import numpy as np
from jax import lax

CX = 16
CY = 16
BLK = 128
OVL = 2
NX = 256
NY = 128
NB_NEW = 256
PAIR_DEV = 512
CAP = 6
PAIRS = 65536
NEW_BLOCKS = 32768
N_CUT = 16
N_DEPTH = 8
DEVICES = 128


def with_ends(values, stream_key, smallest, largest):
    longest = values.shape.index(max(values.shape))
    spots = []
    for shift in (0, 1):
        where = [jax.random.randint(jax.random.fold_in(stream_key, axis), (), 0, length) for axis, length in enumerate(values.shape)]
        where[longest] = (where[longest] + shift) % values.shape[longest]
        spots.append(tuple(where))
    return values.at[spots[0]].set(smallest).at[spots[1]].set(largest)


def level_of(rng, extent, cuts, low, high):
    level, own = 1.0, jax.random.fold_in(rng, 6)
    for axis_at, blocks in cuts:
        heights = jnp.exp(jax.random.uniform(jax.random.fold_in(own, axis_at), (blocks,), jnp.float32, low / len(cuts), high / len(cuts)))
        level = level * jnp.repeat(heights, extent[axis_at] // blocks).reshape([-1 if axis == axis_at else 1 for axis in range(len(extent))])
    return level


def deal_out(key, own, number, rows, count, top, most, slope):
    ranking = jax.random.permutation(key, count)
    heavy_load, ordinary = portions_of(count, rows * top, most, slope, True), portions_of(count, rows * top, most, slope, False)
    places = jnp.arange(count)

    def named(lengths, rotation):
        used = int((lengths > 0).sum())
        fixed = max(1, used // 4)
        shifted = fixed + (places - fixed + rotation * (used - fixed)) % max(1, count - fixed)
        return jnp.zeros((count,), jnp.int32).at[ranking[jnp.where(places < fixed, places, shifted)]].set(jnp.asarray(lengths, jnp.int32))

    lengths = jnp.where(number % 4 == 0, named(heavy_load, number // 4), named(ordinary, number - number // 4 - 1))
    mixed = jax.random.permutation(jax.random.fold_in(own, 3), count)
    donor, sink = mixed[0:count // 2 * 2:2], mixed[1:count // 2 * 2:2]
    room = jnp.minimum(lengths[donor] - 1, most - lengths[sink]) // 2
    room = jnp.where((donor == ranking[0]) | (sink == ranking[0]) | (lengths[sink] == 0), 0, jnp.maximum(room, 0))
    shifted = jax.random.randint(jax.random.fold_in(own, 4), (count // 2,), 0, 1 << 20) % (room + 1)
    lengths = lengths.at[donor].add(-shifted).at[sink].add(shifted)
    labels = jnp.searchsorted(jnp.cumsum(lengths), jnp.arange(rows * top), side="right").astype(jnp.int32)
    grid = labels.reshape(top, rows).T
    grid = grid[jax.random.permutation(jax.random.fold_in(own, 1), rows)]
    rotation = jax.random.randint(jax.random.fold_in(own, 2), (rows, 1), 0, top)
    return jnp.take_along_axis(grid, (jnp.arange(top)[None, :] + rotation) % top, axis=1)


def portions_of(count, total, reach, lean, full):
    weights = [(1 << 20) // math.isqrt(standing ** lean) + 1 for standing in range(1, count + 1)]
    largest = reach if full else min(reach, max(-(-total // count), total * weights[0] // sum(weights)))
    least = 1 if total - largest >= count - 1 else 0
    holding, rest = [largest] + [least] * (count - 1), total - largest - least * (count - 1)
    while rest > 0:
        candidates = [i for i in range(1, count) if holding[i] < largest] or [i for i in range(1, count) if holding[i] < reach]
        pool, remaining = sum([weights[i] for i in candidates]), rest
        for i in candidates:
            extra = min(reach - holding[i], max(1, remaining * weights[i] // pool), rest)
            holding[i] = holding[i] + extra
            rest = rest - extra
    return np.array(holding)


def noise(rng, extent, deviation, bound, cuts=(), held_as=jnp.bfloat16):
    factor_of = level_of(rng, extent, cuts, -0.22, 0.18) if cuts else 1.0
    entries = jax.random.normal(rng, extent, jnp.float32) * deviation * factor_of
    return jnp.minimum(jnp.maximum(entries, -bound), bound).astype(held_as)


def setup_inputs(seed: int = 0) -> dict:
    splits = jax.random.split(jax.random.key(seed), 8)
    initial_state = noise(splits[0], (9, NX, NY, BLK), 1.0, 6.0, ((1, 16), (2, 8)), jnp.float32)
    density = jnp.clip(jnp.exp(math.log(2.0) - 1.3862944 * jax.random.uniform(splits[1], (NX, NY, BLK), jnp.float32) ** level_of(splits[1], (NX, NY, BLK), ((0, 16), (1, 8)), -0.2, 0.2)), 0.5, 2.0)
    yield_flags = with_ends((jax.random.randint(splits[2], (NX, NY), 0, 2) < 1).astype(jnp.int32), jax.random.fold_in(splits[2], 1), 0, 1)
    yield_stress = jnp.clip(jnp.exp(math.log(4.0) - 2.0794415 * jax.random.uniform(splits[3], (NX, NY), jnp.float32) ** level_of(splits[3], (NX, NY), ((0, 16), (1, 8)), -0.2, 0.2)), 0.5, 4.0)
    crossing_weights = jnp.clip(jnp.exp(math.log(0.099609375) - 3.5057412 * jax.random.uniform(splits[4], (PAIRS, BLK, BLK), jnp.float32) ** level_of(splits[4], (PAIRS, BLK, BLK), ((0, 128),), -0.2, 0.2)), 0.0029907227, 0.099609375).astype(jnp.bfloat16)
    new_owner_keys = jax.random.split(jax.random.fold_in(splits[5], 1), PAIRS // PAIR_DEV)
    new_owner_turns = jax.random.permutation(jax.random.fold_in(splits[5], 3), PAIRS // PAIR_DEV)
    new_owner = jax.vmap(lambda own, number: deal_out(jax.random.fold_in(splits[5], 2), own, number, PAIR_DEV, DEVICES, 1, CAP, 2))(new_owner_keys, new_owner_turns).reshape((PAIRS, 1))
    new_slot = with_ends(jax.random.randint(splits[6], (PAIRS,), 0, NB_NEW), jax.random.fold_in(splits[6], 1), 0, NB_NEW - 1).astype(jnp.int32)
    return {"initial_state": initial_state, "density": density, "yield_flags": yield_flags, "yield_stress": yield_stress, "crossing_weights": crossing_weights, "new_owner": new_owner, "new_slot": new_slot}


time_step = 0.15
lame_first = 1.0
shear_modulus = 0.6

def central(values, along_axis):
    widths = [(0, 0)] * values.ndim
    widths[along_axis] = (1, 1)
    padded = jnp.pad(values, widths)
    upper = lax.slice_in_dim(padded, 2, padded.shape[along_axis], axis=along_axis)
    lower = lax.slice_in_dim(padded, 0, padded.shape[along_axis] - 2, axis=along_axis)
    return 0.5 * (upper - lower)

def divergence_of(grads):
    return jnp.stack([grads[0][0] + grads[1][3] + grads[2][5], grads[0][3] + grads[1][1] + grads[2][4], grads[0][5] + grads[1][4] + grads[2][2]])

def plastic_return(stress, grads, yield_flags, yield_stress):
    strain_rate = [grads[0][0], grads[1][1], grads[2][2], 0.5 * (grads[1][0] + grads[0][1]), 0.5 * (grads[2][1] + grads[1][2]), 0.5 * (grads[2][0] + grads[0][2])]
    trace_rate = strain_rate[0] + strain_rate[1] + strain_rate[2]
    trial_stress = []
    for component in range(6):
        update = 2.0 * shear_modulus * strain_rate[component]
        if component < 3:
            update = update + lame_first * trace_rate
        trial_stress.append(stress[component] + time_step * update)
    pressure = (trial_stress[0] + trial_stress[1] + trial_stress[2]) / 3.0
    deviator = [trial_stress[0] - pressure, trial_stress[1] - pressure, trial_stress[2] - pressure, trial_stress[3], trial_stress[4], trial_stress[5]]
    equivalent = jnp.sqrt(1.5 * (deviator[0] ** 2 + deviator[1] ** 2 + deviator[2] ** 2 + 2.0 * (deviator[3] ** 2 + deviator[4] ** 2 + deviator[5] ** 2)))
    limit = yield_stress[:, :, None]
    factor = jnp.where(yield_flags[:, :, None] == 1, limit / jnp.maximum(equivalent, limit), 1.0)
    return jnp.stack([pressure + factor * deviator[0], pressure + factor * deviator[1], pressure + factor * deviator[2], factor * deviator[3], factor * deviator[4], factor * deviator[5]])

def explicit_step(state_field, density, yield_flags, yield_stress):
    velocity_field = state_field[:3]
    stress = state_field[3:]
    stress_grads = [central(stress, 1), central(stress, 2), central(stress, 3)]
    velocity_field = velocity_field + time_step * divergence_of(stress_grads) / density
    velocity_grads = [central(velocity_field, 1), central(velocity_field, 2), central(velocity_field, 3)]
    stress = plastic_return(stress, velocity_grads, yield_flags, yield_stress)
    return jnp.concatenate([velocity_field, stress], 0)

def reference(initial_state, density, yield_flags, yield_stress, crossing_weights, new_owner, new_slot):
    state_field = initial_state
    for turn_index in range(2):
        state_field = explicit_step(state_field, density, yield_flags, yield_stress)
    rounded = lax.optimization_barrier(state_field.astype(jnp.bfloat16)).astype(jnp.float32)
    blocks = rounded.reshape(9, N_CUT, CX, N_DEPTH, CY, BLK).transpose(1, 3, 2, 4, 0, 5)
    blocks = blocks.reshape(DEVICES, CX * CY, 9, BLK)
    weight_blocks = crossing_weights.reshape(DEVICES, CX * CY, OVL, BLK, BLK)
    targets = (new_owner[:, 0] * NB_NEW + new_slot).astype(jnp.int32).reshape(DEVICES, PAIR_DEV)

    def accumulate(total, pieces):
        block_fields, block_weights, block_targets = pieces
        contribution = jnp.einsum('bci,boij->bocj', block_fields, block_weights.astype(jnp.float32))
        contribution = contribution.reshape(PAIR_DEV, 9, BLK)
        return (total.at[block_targets].add(contribution), None)
    total, unused = lax.scan(accumulate, jnp.zeros((NEW_BLOCKS, 9, BLK), jnp.float32), (blocks, weight_blocks, targets))
    return (state_field, total)
```

```python
import jax
import jax.numpy as jnp
from jax import lax
from jax.experimental import pallas as pl
from jax.experimental.pallas import tpu as pltpu
from jax.sharding import PartitionSpec as P

f32 = jnp.float32
N = 16
R = 4
E = N + 2 * R
W = 128
DEV = 128
CAP = 6
TILES = CAP + 1
SLABS = 6 * 4 + 3 * 3 + 3 + 2
INNER = 22
DEP = INNER * 4
DEPTH_ROWS = 10 * DEP + 40
SLOTS = 256
VMEM_LIMIT = 52 * 1024 * 1024
BIG = 1e30


def slab_of(field, offset):
    if field < 6:
        return field * 4 + offset
    if field < 9:
        return 24 + (field - 6) * 3 + offset
    if field == 9:
        return 33 + offset
    return 36 + offset


def reach_of(field):
    return 4 if field < 6 else (3 if field < 10 else 2)


def own_row(field, row, state_ref, inv, limit_ref):
    if field < 6:
        return state_ref[3 + field, row]
    if field < 9:
        return state_ref[field - 6, row]
    if field == 9:
        return inv(row)
    return limit_ref[row]


def pack_cut(state_ref, density_ref, limit_ref, low_ref, high_ref):
    def inv(row):
        return 0.075 / density_ref[row]

    for field in range(11):
        reach = reach_of(field)
        for offset in range(reach):
            low_ref[slab_of(field, offset)] = own_row(field, offset, state_ref, inv, limit_ref)
            high_ref[slab_of(field, offset)] = own_row(
                field, N - reach + offset, state_ref, inv, limit_ref
            )


def extended_row(field, r, state_ref, inv, limit_ref, from_low_ref, from_high_ref):
    if r < R:
        return from_low_ref[slab_of(field, r - (R - reach_of(field)))]
    if r >= R + N:
        return from_high_ref[slab_of(field, r - R - N)]
    return own_row(field, r - R, state_ref, inv, limit_ref)


def pack_depth(state_ref, density_ref, limit_ref, from_low_ref, from_high_ref, low_ref, high_ref):
    def inv(row):
        return 0.075 / density_ref[row]

    for field in range(10):
        for r in range(1, 1 + INNER):
            row = extended_row(field, r, state_ref, inv, limit_ref, from_low_ref, from_high_ref)
            at = field * DEP + (r - 1) * 4
            low_ref[at : at + 4] = row[:4]
            high_ref[at : at + 4] = row[12:]
    for r in range(3, 21):
        row = extended_row(10, r, state_ref, inv, limit_ref, from_low_ref, from_high_ref)
        at = 10 * DEP + (r - 3) * 2
        low_ref[at : at + 2] = row[:2]
        high_ref[at : at + 2] = row[14:]


def steps_and_remap(
    place_ref,
    state_ref,
    density_ref,
    limit_ref,
    cut_low_ref,
    cut_high_ref,
    depth_low_ref,
    depth_high_ref,
    labels_ref,
    weights_ref,
    after_ref,
    outgoing_ref,
    ext,
    rows,
    held,
    sems,
):
    per = 2 * N

    def fetch(cx):
        return pltpu.make_async_copy(
            weights_ref.at[pl.ds(cx * per, per)], held.at[pl.ds(cx * per, per)], sems.at[cx]
        )

    for cx in range(N):
        fetch(cx).start()

    def inv(row):
        return 0.075 / density_ref[row]

    zeros4 = jnp.zeros((4, W), f32)
    zeros2 = jnp.zeros((2, W), f32)
    for field in range(11):
        reach = reach_of(field)
        for r in range(R - reach, R + N + reach):
            row = extended_row(field, r, state_ref, inv, limit_ref, cut_low_ref, cut_high_ref)
            if field < 10 and 1 <= r <= INNER:
                at = field * DEP + (r - 1) * 4
                low, high = depth_low_ref[at : at + 4], depth_high_ref[at : at + 4]
            elif field == 10 and 3 <= r <= 20:
                at = 10 * DEP + (r - 3) * 2
                low = jnp.concatenate([zeros2, depth_low_ref[at : at + 2]], 0)
                high = jnp.concatenate([depth_high_ref[at : at + 2], zeros2], 0)
            else:
                low = high = zeros4
            ext[field, r] = jnp.concatenate([low, row, high], 0)

    def label(owner, carry):
        outgoing_ref[owner * TILES + CAP] = jnp.broadcast_to(labels_ref[owner], (8, W))
        return carry

    lax.fori_loop(0, DEV, label, 0)

    lane = lax.broadcasted_iota(jnp.int32, (E, W), 1)
    first, last = lane == 0, lane == W - 1

    def along_depth(x):
        return pltpu.roll(x, E - 1, 0) - pltpu.roll(x, 1, 0)

    def along_width(x):
        up = jnp.where(last, 0.0, pltpu.roll(x, W - 1, 1))
        down = jnp.where(first, 0.0, pltpu.roll(x, 1, 1))
        return up - down

    def velocity(r, carry):
        def along_cut(field):
            return ext[field, r + 1] - ext[field, r - 1]

        scale = ext[9, r]
        xy, yz, xz = ext[3, r], ext[4, r], ext[5, r]
        ext[6, r] += (along_cut(0) + along_depth(xy) + along_width(xz)) * scale
        ext[7, r] += (along_cut(3) + along_depth(ext[1, r]) + along_width(yz)) * scale
        ext[8, r] += (along_cut(5) + along_depth(yz) + along_width(ext[2, r])) * scale
        return carry

    def stress(r):
        vx, vy, vz = ext[6, r], ext[7, r], ext[8, r]
        limit = ext[10, r]

        def along_cut(field):
            return ext[field, r + 1] - ext[field, r - 1]

        xx, yy, zz = along_cut(6), along_depth(vy), along_width(vz)
        bulk = 0.075 * (xx + yy + zz)
        sxx = ext[0, r] + (0.09 * xx + bulk)
        syy = ext[1, r] + (0.09 * yy + bulk)
        szz = ext[2, r] + (0.09 * zz + bulk)
        sxy = ext[3, r] + 0.045 * (along_depth(vx) + along_cut(7))
        syz = ext[4, r] + 0.045 * (along_width(vy) + along_depth(vz))
        sxz = ext[5, r] + 0.045 * (along_width(vx) + along_cut(8))
        p = (sxx + syy + szz) * (1.0 / 3.0)
        dxx, dyy, dzz = sxx - p, syy - p, szz - p
        square = 1.5 * (
            dxx * dxx + dyy * dyy + dzz * dzz + 2.0 * (sxy * sxy + syz * syz + sxz * sxz)
        )
        factor = jnp.minimum(1.0, limit * lax.rsqrt(square))
        inside = limit > 0.0
        new = (
            p + factor * dxx,
            p + factor * dyy,
            p + factor * dzz,
            factor * sxy,
            factor * syz,
            factor * sxz,
        )
        return [jnp.where(inside, x, 0.0) for x in new]

    def stress_loop(r, carry):
        for field, x in enumerate(stress(r)):
            ext[field, r] = x
        return carry

    lax.fori_loop(1, 23, velocity, 0)
    lax.fori_loop(2, 22, stress_loop, 0)
    lax.fori_loop(3, 21, velocity, 0)

    def remap(cx, carry):
        r = cx + R
        fields = [ext[6, r], ext[7, r], ext[8, r]] + stress(r)
        for field, x in enumerate(fields):
            own = x[R : R + N]
            after_ref[field, cx] = own
            rows[pl.ds(field, N, stride=16)] = own
        fetch(cx).wait()
        for cy in range(N):
            block = rows[cy * 16 : (cy + 1) * 16].astype(jnp.bfloat16)
            for crossing in range(2):
                pair = cx * per + 2 * cy + crossing
                result = jnp.dot(block, held[pair], preferred_element_type=f32)
                place = place_ref[pair]
                base = (place >> 3) * TILES
                rank = place & 7
                outgoing_ref[base + rank] = result[:8]
                outgoing_ref[base + CAP, pl.ds(rank, 1)] = result[8:9]
        return carry

    lax.fori_loop(0, N, remap, 0)


PARTS = 3
ROOM = SLOTS + 8


def gather(slots_ref, arrived_ref, out_ref, *sums):
    main, rest = sums[:PARTS], sums[PARTS:]
    for k in range(PARTS):
        main[k][...] = jnp.zeros((8 * ROOM, W), f32)
        rest[k][...] = jnp.zeros((ROOM, W), f32)

    def add(source, carry):
        for k in range(CAP):
            slot = slots_ref[source * CAP + k]
            part = k % PARTS
            tile = pl.ds(pl.multiple_of(slot * 8, 8), 8)
            main[part][tile] += arrived_ref[source * TILES + k]
            rest[part][pl.ds(slot, 1)] += arrived_ref[source * TILES + CAP, k : k + 1]
        return carry

    lax.fori_loop(0, DEV, add, 0)
    for field in range(8):
        spot = pl.ds(field, SLOTS, stride=8)
        out_ref[field] = main[0][spot] + main[1][spot] + main[2][spot]
    out_ref[8] = rest[0][:SLOTS] + rest[1][:SLOTS] + rest[2][:SLOTS]


def exchange(low, high, axis):
    count = lax.axis_size(axis)
    up = [(i, i + 1) for i in range(count - 1)]
    down = [(target, source) for source, target in up]
    return lax.ppermute(high, axis, up), lax.ppermute(low, axis, down)


VM = pl.BlockSpec(memory_space=pltpu.VMEM)
SM = pl.BlockSpec(memory_space=pltpu.SMEM)
HB = pl.BlockSpec(memory_space=pl.ANY)
PARAMS = pltpu.CompilerParams(vmem_limit_bytes=VMEM_LIMIT)


def on_device(
    initial_state, density, yield_flags, yield_stress, crossing_weights, new_owner, new_slot
):
    limit = jnp.broadcast_to(
        jnp.where(yield_flags == 1, yield_stress, BIG)[:, :, None], (N, N, W)
    )
    cut_shape = jax.ShapeDtypeStruct((SLABS, N, W), f32)
    low, high = pl.pallas_call(
        pack_cut,
        out_shape=(cut_shape, cut_shape),
        in_specs=[VM] * 3,
        out_specs=(VM, VM),
        compiler_params=PARAMS,
        name="pack_cut",
    )(initial_state, density, limit)
    cut_low, cut_high = exchange(low, high, "cut")
    depth_shape = jax.ShapeDtypeStruct((DEPTH_ROWS, W), f32)
    low, high = pl.pallas_call(
        pack_depth,
        out_shape=(depth_shape, depth_shape),
        in_specs=[VM] * 5,
        out_specs=(VM, VM),
        compiler_params=PARAMS,
        name="pack_depth",
    )(initial_state, density, limit, cut_low, cut_high)
    depth_low, depth_high = exchange(low, high, "depth")

    owners = new_owner[:, 0]
    hits = (owners[:, None] == jnp.arange(DEV, dtype=jnp.int32)[None, :]).astype(jnp.int32)
    rank = jnp.sum((jnp.cumsum(hits, 0) - hits) * hits, 1)
    place = owners * 8 + rank
    by_rank = jnp.where(
        rank[:, None] == jnp.arange(W, dtype=jnp.int32)[None, :], new_slot[:, None] + 1, 0
    )
    labels = lax.dot_general(
        hits.astype(jnp.bfloat16),
        by_rank.astype(jnp.bfloat16),
        (((0,), (0,)), ((), ())),
        preferred_element_type=f32,
    )

    state_after, outgoing = pl.pallas_call(
        steps_and_remap,
        out_shape=(
            jax.ShapeDtypeStruct((9, N, N, W), f32),
            jax.ShapeDtypeStruct((DEV * TILES, 8, W), f32),
        ),
        in_specs=[SM] + [VM] * 8 + [HB],
        out_specs=(VM, VM),
        scratch_shapes=[
            pltpu.VMEM((11, E, E, W), f32),
            pltpu.VMEM((N * 16, W), f32),
            pltpu.VMEM((2 * N * N, W, W), jnp.bfloat16),
            pltpu.SemaphoreType.DMA((N,)),
        ],
        compiler_params=PARAMS,
        name="steps_and_remap",
    )(
        place,
        initial_state,
        density,
        limit,
        cut_low,
        cut_high,
        depth_low,
        depth_high,
        labels[:, None, :],
        crossing_weights,
    )
    arrived = lax.all_to_all(outgoing, ("cut", "depth"), split_axis=0, concat_axis=0, tiled=True)
    slots = arrived.reshape(DEV, TILES, 8, W)[:, CAP, CAP, :CAP].astype(jnp.int32).reshape(-1)
    slots = jnp.where(slots == 0, SLOTS, slots - 1)
    new_integrals = pl.pallas_call(
        gather,
        out_shape=jax.ShapeDtypeStruct((9, SLOTS, W), f32),
        in_specs=[SM, VM],
        out_specs=VM,
        scratch_shapes=[pltpu.VMEM((8 * ROOM, W), f32)] * PARTS
        + [pltpu.VMEM((ROOM, W), f32)] * PARTS,
        compiler_params=PARAMS,
        name="gather",
    )(slots, arrived)
    return (state_after, new_integrals.transpose(1, 0, 2))


def solution(mesh):
    return jax.shard_map(
        on_device,
        mesh=mesh,
        in_specs=(
            P(None, "cut", "depth", None),
            P("cut", "depth", None),
            P("cut", "depth"),
            P("cut", "depth"),
            P(("cut", "depth"), None, None),
            P(("cut", "depth"), None),
            P(("cut", "depth")),
        ),
        out_specs=(P(None, "cut", "depth", None), P(("cut", "depth"), None, None)),
        check_vma=False,
    )
```

```python
import jax
import jax.numpy as jnp
from jax import lax
from jax.experimental import pallas as pl
from jax.experimental.pallas import tpu as pltpu
from jax.sharding import PartitionSpec as P

f32 = jnp.float32
N = 16
R = 4
E = N + 2 * R
W = 128
DEV = 128
CAP = 6
TILES = CAP + 1
SLOTS = 256
BIG = 1e30
MIB = 1024 * 1024

REACH = (4, 3, 3, 4, 3, 4, 3, 3, 3, 3, 2)
STARTS = tuple(sum(REACH[:field]) for field in range(10))
LIMIT_SLAB = sum(REACH[:10])
SLABS = LIMIT_SLAB + 1
SIDE = 4 * N
SIDE_ROWS = 11 * SIDE
CORNER = 4 * 6
CORNER_ROWS = 10 * CORNER + 8


def limit_row(flags_ref, stress_ref, row):
    along = jnp.where(
        flags_ref[row : row + 1] == 1, stress_ref[row : row + 1], BIG
    )
    square = jnp.broadcast_to(along, (N, N))
    diagonal = lax.broadcasted_iota(jnp.int32, (N, N), 0) == lax.broadcasted_iota(
        jnp.int32, (N, N), 1
    )
    column = jnp.sum(jnp.where(diagonal, square, 0.0), axis=1, keepdims=True)
    return jnp.broadcast_to(column, (N, W))


def scaled_inverse(density):
    return 0.075 / density


def pack_cut(
    flags_hbm, stress_hbm, state_ref, density_ref, low_ref, high_ref, flags_ref, stress_ref, edges, sems
):
    copies = [
        pltpu.make_async_copy(flags_hbm, flags_ref, sems.at[20]),
        pltpu.make_async_copy(stress_hbm, stress_ref, sems.at[21]),
    ]
    for field in range(9):
        source = state_ref.at[3 + field if field < 6 else field - 6]
        reach, start = REACH[field], STARTS[field]
        for side, target in enumerate((low_ref, high_ref)):
            copies.append(
                pltpu.make_async_copy(
                    source.at[pl.ds(side * (N - reach), reach)],
                    target.at[pl.ds(start, reach)],
                    sems.at[2 * field + side],
                )
            )
    for side in range(2):
        copies.append(
            pltpu.make_async_copy(
                density_ref.at[pl.ds(side * (N - 3), 3)], edges.at[side], sems.at[18 + side]
            )
        )
    for copy in copies:
        copy.start()
    copies[0].wait()
    copies[1].wait()
    half = lax.broadcasted_iota(jnp.int32, (N, W), 1) < W // 2
    for side, target in enumerate((low_ref, high_ref)):
        at = side * (N - 2)
        target[LIMIT_SLAB] = jnp.where(
            half,
            limit_row(flags_ref, stress_ref, at),
            limit_row(flags_ref, stress_ref, at + 1),
        )
    for copy in copies[2:]:
        copy.wait()
    for side, target in enumerate((low_ref, high_ref)):
        for row in range(3):
            target[STARTS[9] + row] = scaled_inverse(edges[side, row])


def pack_depth(flags_ref, stress_ref, state_ref, density_ref, low_ref, high_ref):
    for field in range(11):
        for row in range(N):
            if field < 6:
                own = state_ref[3 + field, row]
            elif field < 9:
                own = state_ref[field - 6, row]
            elif field == 9:
                own = scaled_inverse(density_ref[row])
            else:
                own = limit_row(flags_ref, stress_ref, row)
            at = field * SIDE + row * 4
            low_ref[at : at + 4] = own[:4]
            high_ref[at : at + 4] = own[N - 4 :]


def cut_row(field, r, from_low_ref, from_high_ref):
    source = from_low_ref if r < R else from_high_ref
    if field == 10:
        slab = source[LIMIT_SLAB]
        first = lax.broadcasted_iota(jnp.int32, (N, W), 1) < W // 2
        wanted = first if r in (R - 2, R + N) else ~first
        return jnp.where(wanted, slab, pltpu.roll(slab, W // 2, 1))
    return source[STARTS[field] + (r - (R - REACH[field]) if r < R else r - R - N)]


def corner_at(field, r):
    if field == 10:
        return 10 * CORNER + (0 if r < R else 4)
    return field * CORNER + 4 * (r - 1 if r < R else r - R - N + 3)


def corner_rows(field):
    return (3, 20) if field == 10 else (1, 2, 3, 20, 21, 22)


def pack_corners(from_low_ref, from_high_ref, low_ref, high_ref):
    for field in range(11):
        for r in corner_rows(field):
            row = cut_row(field, r, from_low_ref, from_high_ref)
            at = corner_at(field, r)
            low_ref[at : at + 4] = row[:4]
            high_ref[at : at + 4] = row[N - 4 :]


def steps_and_remap(
    place_ref,
    flags_ref,
    yield_ref,
    state_ref,
    density_ref,
    cut_low_ref,
    cut_high_ref,
    side_low_ref,
    side_high_ref,
    corner_low_ref,
    corner_high_ref,
    labels_ref,
    weights_ref,
    after_ref,
    outgoing_ref,
    tension,
    velocity,
    inverse,
    limits,
    rows,
    after,
    held,
    sems,
    after_sem,
):
    per = 2 * N

    def fetch(cx):
        return pltpu.make_async_copy(
            weights_ref.at[pl.ds(cx * per, per)], held.at[pl.ds(cx * per, per)], sems.at[cx]
        )

    for cx in range(N):
        fetch(cx).start()

    for field in range(11):
        reach = REACH[field]
        for r in range(R - reach, R + N + reach):
            if r < R or r >= R + N:
                own = cut_row(field, r, cut_low_ref, cut_high_ref)
            elif field < 6:
                own = state_ref[3 + field, r - R]
            elif field < 9:
                own = state_ref[field - 6, r - R]
            elif field == 9:
                own = scaled_inverse(density_ref[r - R])
            else:
                own = limit_row(flags_ref, yield_ref, r - R)
            if R <= r < R + N:
                at = field * SIDE + 4 * (r - R)
                beside = (side_high_ref[at : at + 4], side_low_ref[at : at + 4])
            elif r in corner_rows(field):
                at = corner_at(field, r)
                beside = (corner_high_ref[at : at + 4], corner_low_ref[at : at + 4])
            else:
                beside = (jnp.zeros((8, W), f32),)
            if field < 6:
                target = tension.at[field, r]
            elif field < 9:
                target = velocity.at[field - 6, r]
            else:
                target = (inverse if field == 9 else limits).at[r]
            target[:N] = own
            target[N:] = jnp.concatenate(beside, 0)

    def label(i, carry):
        for j in range(8):
            owner = i * 8 + j
            outgoing_ref[owner * TILES + CAP] = jnp.broadcast_to(labels_ref[owner], (8, W))
        return carry

    lax.fori_loop(0, DEV // 8, label, 0)

    lane = lax.broadcasted_iota(jnp.int32, (E, W), 1)
    first, last = lane == 0, lane == W - 1

    def along_depth(x):
        return pltpu.roll(x, E - 1, 0) - pltpu.roll(x, 1, 0)

    def along_width(x):
        up = jnp.where(last, 0.0, pltpu.roll(x, W - 1, 1))
        down = jnp.where(first, 0.0, pltpu.roll(x, 1, 1))
        return up - down

    def new_velocity(r):
        def along_cut(field):
            return tension[field, r + 1] - tension[field, r - 1]

        scale = inverse[r]
        xy, yz, xz = tension[3, r], tension[4, r], tension[5, r]
        return (
            velocity[0, r] + (along_cut(0) + along_depth(xy) + along_width(xz)) * scale,
            velocity[1, r] + (along_cut(3) + along_depth(tension[1, r]) + along_width(yz)) * scale,
            velocity[2, r] + (along_cut(5) + along_depth(yz) + along_width(tension[2, r])) * scale,
        )

    def new_stress(r):
        vx, vy, vz = velocity[0, r], velocity[1, r], velocity[2, r]
        limit = limits[r]

        def along_cut(field):
            return velocity[field, r + 1] - velocity[field, r - 1]

        xx, yy, zz = along_cut(0), along_depth(vy), along_width(vz)
        bulk = 0.075 * (xx + yy + zz)
        sxx = tension[0, r] + (0.09 * xx + bulk)
        syy = tension[1, r] + (0.09 * yy + bulk)
        szz = tension[2, r] + (0.09 * zz + bulk)
        sxy = tension[3, r] + 0.045 * (along_depth(vx) + along_cut(1))
        syz = tension[4, r] + 0.045 * (along_width(vy) + along_depth(vz))
        sxz = tension[5, r] + 0.045 * (along_width(vx) + along_cut(2))
        p = (sxx + syy + szz) * (1.0 / 3.0)
        dxx, dyy, dzz = sxx - p, syy - p, szz - p
        square = 1.5 * (
            dxx * dxx + dyy * dyy + dzz * dzz + 2.0 * (sxy * sxy + syz * syz + sxz * sxz)
        )
        factor = jnp.minimum(1.0, limit * lax.rsqrt(square))
        inside = limit > 0.0
        new = (
            p + factor * dxx,
            p + factor * dyy,
            p + factor * dzz,
            factor * sxy,
            factor * syz,
            factor * sxz,
        )
        return [jnp.where(inside, x, 0.0) for x in new]

    def sweep(start, stop, update, target):
        def body(i, carry):
            at = [start + GROUP * i + j for j in range(GROUP)]
            results = [update(r) for r in at]
            for r, result in zip(at, results):
                for field, x in enumerate(result):
                    target[field, r] = x
            return carry

        whole = (stop - start) // GROUP
        lax.fori_loop(0, whole, body, 0)
        rest = range(start + whole * GROUP, stop)
        for r, result in zip(rest, [update(r) for r in rest]):
            for field, x in enumerate(result):
                target[field, r] = x

    sweep(1, 23, new_velocity, velocity)
    sweep(2, 22, new_stress, tension)
    sweep(3, 21, new_velocity, velocity)

    def finish(i, carry):
        at = [GROUP * i + j for j in range(GROUP)]
        results = [new_stress(cx + R) for cx in at]
        for cx, result in zip(at, results):
            fields = [velocity[f, cx + R] for f in range(3)] + result
            for field, x in enumerate(fields):
                own = x[:N]
                after[field, cx] = own
                rows[cx, pl.ds(field, N, stride=16)] = own
        return carry

    lax.fori_loop(0, N // GROUP, finish, 0)
    keep = pltpu.make_async_copy(after, after_ref, after_sem)
    keep.start()

    def remap(cx, carry):
        fetch(cx).wait()
        for cy in range(0, N, 2):
            one = rows[cx, cy * 16 : (cy + 1) * 16].astype(jnp.bfloat16)
            two = rows[cx, (cy + 1) * 16 : (cy + 2) * 16].astype(jnp.bfloat16)
            none = jnp.zeros((16, W), jnp.bfloat16)
            blocks = jnp.concatenate(
                [jnp.concatenate([one, none], 1), jnp.concatenate([none, two], 1)], 0
            )
            pair = cx * per + 2 * cy
            spread = jnp.concatenate(
                [
                    jnp.concatenate([held[pair], held[pair + 1]], 1),
                    jnp.concatenate([held[pair + 2], held[pair + 3]], 1),
                ],
                0,
            )
            result = jnp.dot(blocks, spread, preferred_element_type=f32)
            for k in range(4):
                place = place_ref[pair + k]
                base = (place >> 3) * TILES
                rank = place & 7
                part = result[16 * (k // 2) : 16 * (k // 2) + 9, W * (k % 2) : W * (k % 2 + 1)]
                outgoing_ref[base + rank] = part[:8]
                outgoing_ref[base + CAP, pl.ds(rank, 1)] = part[8:9]
        return carry

    lax.fori_loop(0, N, remap, 0)
    keep.wait()


GROUP = 4
PARTS = 6
ROOM = SLOTS + 8


def gather(arrived, out_ref, turned, slots, sem, *sums):
    main, rest = sums[:PARTS], sums[PARTS:]
    named = arrived[:, CAP, CAP, :].T[:8].astype(jnp.int32)
    turned[...] = jnp.where(named == 0, SLOTS, named - 1)
    copy = pltpu.make_async_copy(turned, slots, sem)
    copy.start()
    for k in range(PARTS):
        main[k][...] = jnp.zeros((8 * ROOM, W), f32)
        rest[k][...] = jnp.zeros((ROOM, W), f32)
    copy.wait()

    def sources(i, carry):
        for j in range(UNROLL):
            source = i * UNROLL + j
            for k in range(CAP):
                slot = slots[k, source]
                tile = pl.ds(pl.multiple_of(slot * 8, 8), 8)
                main[k][tile] += arrived[source, k]
                rest[k][pl.ds(slot, 1)] += arrived[source, CAP, k : k + 1]
        return carry

    lax.fori_loop(0, DEV // UNROLL, sources, 0)

    def total(parts, spot):
        one, two, three = (parts[k][spot] + parts[k + 3][spot] for k in range(3))
        return one + two + three

    def fold(i, carry):
        spot = pl.ds(pl.multiple_of(i * W, W), W)
        main[0][spot] = total(main, spot)
        return carry

    lax.fori_loop(0, 8 * SLOTS // W, fold, 0)
    for field in range(8):
        out_ref[field] = main[0][pl.ds(field, SLOTS, stride=8)]
    out_ref[8] = total(rest, pl.ds(0, SLOTS))


UNROLL = 4


def exchange(low, high, axis):
    count = lax.axis_size(axis)
    up = [(i, i + 1) for i in range(count - 1)]
    down = [(target, source) for source, target in up]
    return lax.ppermute(high, axis, up), lax.ppermute(low, axis, down)


VM = pl.BlockSpec(memory_space=pltpu.VMEM)
SM = pl.BlockSpec(memory_space=pltpu.SMEM)
HB = pl.BlockSpec(memory_space=pltpu.HBM)
SMALL = pltpu.CompilerParams(vmem_limit_bytes=8 * MIB)


def stay(x):
    return pltpu.with_memory_space_constraint(x, pltpu.HBM)


def both(rows):
    return (jax.ShapeDtypeStruct(rows + (W,), f32),) * 2


def on_device(
    initial_state, density, yield_flags, yield_stress, crossing_weights, new_owner, new_slot
):
    low, high = pl.pallas_call(
        pack_cut,
        out_shape=both((SLABS, N)),
        in_specs=[HB] * 4,
        out_specs=(VM, VM),
        scratch_shapes=[
            pltpu.VMEM((N, N), jnp.int32),
            pltpu.VMEM((N, N), f32),
            pltpu.VMEM((2, 3, N, W), f32),
            pltpu.SemaphoreType.DMA((22,)),
        ],
        compiler_params=SMALL,
        name="pack_cut",
    )(*(stay(x) for x in (yield_flags, yield_stress, initial_state, density)))
    cut_low, cut_high = exchange(low, high, "cut")
    low, high = pl.pallas_call(
        pack_depth,
        out_shape=both((SIDE_ROWS,)),
        in_specs=[VM] * 4,
        out_specs=(VM, VM),
        compiler_params=SMALL,
        name="pack_depth",
    )(yield_flags, yield_stress, initial_state, density)
    side_low, side_high = exchange(low, high, "depth")
    low, high = pl.pallas_call(
        pack_corners,
        out_shape=both((CORNER_ROWS,)),
        in_specs=[VM] * 2,
        out_specs=(VM, VM),
        compiler_params=SMALL,
        name="pack_corners",
    )(cut_low, cut_high)
    corner_low, corner_high = exchange(low, high, "depth")

    owners = new_owner[:, 0]
    hits = (owners[:, None] == jnp.arange(DEV, dtype=jnp.int32)[None, :]).astype(jnp.int32)
    rank = jnp.sum((jnp.cumsum(hits, 0) - hits) * hits, 1)
    place = owners * 8 + rank
    by_rank = jnp.where(
        rank[:, None] == jnp.arange(W, dtype=jnp.int32)[None, :], new_slot[:, None] + 1, 0
    )
    labels = lax.dot_general(
        hits.astype(jnp.bfloat16),
        by_rank.astype(jnp.bfloat16),
        (((0,), (0,)), ((), ())),
        preferred_element_type=f32,
    )

    state_after, outgoing = pl.pallas_call(
        steps_and_remap,
        out_shape=(
            jax.ShapeDtypeStruct((9, N, N, W), f32),
            jax.ShapeDtypeStruct((DEV * TILES, 8, W), f32),
        ),
        in_specs=[SM] + [VM] * 11 + [HB],
        out_specs=(HB, VM),
        scratch_shapes=[
            pltpu.VMEM((6, E, E, W), f32),
            pltpu.VMEM((3, E, E, W), f32),
            pltpu.VMEM((E, E, W), f32),
            pltpu.VMEM((E, E, W), f32),
            pltpu.VMEM((N, N * 16, W), f32),
            pltpu.VMEM((9, N, N, W), f32),
            pltpu.VMEM((2 * N * N, W, W), jnp.bfloat16),
            pltpu.SemaphoreType.DMA((N,)),
            pltpu.SemaphoreType.DMA,
        ],
        compiler_params=pltpu.CompilerParams(vmem_limit_bytes=40 * MIB),
        name="steps_and_remap",
    )(
        place,
        yield_flags,
        yield_stress,
        initial_state,
        density,
        cut_low,
        cut_high,
        side_low,
        side_high,
        corner_low,
        corner_high,
        labels[:, None, :],
        stay(crossing_weights),
    )
    arrived = lax.all_to_all(outgoing, ("cut", "depth"), split_axis=0, concat_axis=0, tiled=True)
    new_integrals = pl.pallas_call(
        gather,
        out_shape=jax.ShapeDtypeStruct((9, SLOTS, W), f32),
        in_specs=[VM],
        out_specs=VM,
        scratch_shapes=[
            pltpu.VMEM((8, W), jnp.int32),
            pltpu.SMEM((8, W), jnp.int32),
            pltpu.SemaphoreType.DMA,
        ]
        + [pltpu.VMEM((8 * ROOM, W), f32)] * PARTS
        + [pltpu.VMEM((ROOM, W), f32)] * PARTS,
        compiler_params=pltpu.CompilerParams(vmem_limit_bytes=24 * MIB),
        name="gather",
    )(arrived.reshape(DEV, TILES, 8, W))
    return (state_after, new_integrals.transpose(1, 0, 2))


def solution(mesh):
    return jax.shard_map(
        on_device,
        mesh=mesh,
        in_specs=(
            P(None, "cut", "depth", None),
            P("cut", "depth", None),
            P("cut", "depth"),
            P("cut", "depth"),
            P(("cut", "depth"), None, None),
            P(("cut", "depth"), None),
            P(("cut", "depth")),
        ),
        out_specs=(P(None, "cut", "depth", None), P(("cut", "depth"), None, None)),
        check_vma=False,
    )
```

```python
import jax
import jax.numpy as jnp
from jax import lax
from jax.experimental import pallas as pl
from jax.experimental.pallas import tpu as pltpu
from jax.sharding import PartitionSpec as P

f32 = jnp.float32
N = 16
R = 4
E = N + 2 * R
W = 128
DEV = 128
CAP = 6
TILES = CAP + 1
SLOTS = 256
BIG = 1e30
MIB = 1024 * 1024

REACH = (4, 3, 3, 4, 3, 4, 3, 3, 3, 3, 2)
STARTS = tuple(sum(REACH[:field]) for field in range(10))
LIMIT_SLAB = sum(REACH[:10])
SLABS = LIMIT_SLAB + 1
WIDTH = (3, 4, 3, 4, 4, 3, 3, 3, 3, 3, 2)
RADIUS = (4,) * 6 + (3,) * 4 + (2,)


def pieces(corners, at):
    found = {}
    for field in range(11):
        for r in range(E):
            beyond = max(R - r, r - (R + N - 1), 0)
            width = WIDTH[field] if beyond == 0 else RADIUS[field] - beyond
            if width > 0 and (beyond > 0) == corners:
                found[field, r] = (width, at)
                at += width
    return found, at


BESIDE, BESIDE_ROWS = pieces(False, 0)
CORNERS, PIECE_ROWS = pieces(True, BESIDE_ROWS)
PIECES = BESIDE | CORNERS
SIDE_ROWS = -(-PIECE_ROWS // 8) * 8


def is_odd(axis):
    return lax.rem(lax.axis_index(axis), 2) == 1


def limit_row(flags_ref, stress_ref, row):
    along = jnp.where(
        flags_ref[row : row + 1] == 1, stress_ref[row : row + 1], BIG
    )
    square = jnp.broadcast_to(along, (N, N))
    diagonal = lax.broadcasted_iota(jnp.int32, (N, N), 0) == lax.broadcasted_iota(
        jnp.int32, (N, N), 1
    )
    column = jnp.sum(jnp.where(diagonal, square, 0.0), axis=1, keepdims=True)
    return jnp.broadcast_to(column, (N, W))


def scaled_inverse(density):
    return 0.075 / density


def pack_cut(
    flags_hbm, stress_hbm, state_ref, density_ref, one_ref, two_ref, flags_ref, stress_ref, edges, sems
):
    odd = lax.rem(lax.axis_index("cut"), 2)
    tops = ((one_ref, odd), (two_ref, 1 - odd))
    copies = [
        pltpu.make_async_copy(flags_hbm, flags_ref, sems.at[20]),
        pltpu.make_async_copy(stress_hbm, stress_ref, sems.at[21]),
    ]
    for field in range(9):
        source = state_ref.at[3 + field if field < 6 else field - 6]
        reach, start = REACH[field], STARTS[field]
        for side, (target, top) in enumerate(tops):
            copies.append(
                pltpu.make_async_copy(
                    source.at[pl.ds(top * (N - reach), reach)],
                    target.at[pl.ds(start, reach)],
                    sems.at[2 * field + side],
                )
            )
    for side, (target, top) in enumerate(tops):
        copies.append(
            pltpu.make_async_copy(
                density_ref.at[pl.ds(top * (N - 3), 3)], edges.at[side], sems.at[18 + side]
            )
        )
    for copy in copies:
        copy.start()
    copies[0].wait()
    copies[1].wait()
    half = lax.broadcasted_iota(jnp.int32, (N, W), 1) < W // 2
    slabs = [
        jnp.where(
            half,
            limit_row(flags_ref, stress_ref, row),
            limit_row(flags_ref, stress_ref, row + 1),
        )
        for row in (0, N - 2)
    ]
    for target, top in tops:
        target[LIMIT_SLAB] = jnp.where(top == 1, slabs[1], slabs[0])
    for copy in copies[2:]:
        copy.wait()
    for side, (target, top) in enumerate(tops):
        for row in range(3):
            target[STARTS[9] + row] = scaled_inverse(edges[side, row])


def cut_row(field, r, odd, one_ref, two_ref):
    def came(slab):
        one, two = one_ref[slab], two_ref[slab]
        return jnp.where(odd, two, one) if r < R else jnp.where(odd, one, two)

    if field == 10:
        slab = came(LIMIT_SLAB)
        first = lax.broadcasted_iota(jnp.int32, (N, W), 1) < W // 2
        wanted = first if r in (R - 2, R + N) else ~first
        return jnp.where(wanted, slab, pltpu.roll(slab, W // 2, 1))
    return came(STARTS[field] + (r - (R - REACH[field]) if r < R else r - R - N))


def own_row(field, row, flags_ref, yield_ref, state_ref, density_ref):
    if field < 6:
        return state_ref[3 + field, row]
    if field < 9:
        return state_ref[field - 6, row]
    if field == 9:
        return scaled_inverse(density_ref[row])
    return limit_row(flags_ref, yield_ref, row)


def put_piece(row, width, at, odd, one_ref, two_ref):
    low, high = row[:width], row[N - width :]
    one_ref[at : at + width] = jnp.where(odd, high, low)
    two_ref[at : at + width] = jnp.where(odd, low, high)


def pack_beside(
    flags_hbm,
    yield_hbm,
    state_hbm,
    density_hbm,
    one_ref,
    two_ref,
    flags_ref,
    yield_ref,
    state_ref,
    density_ref,
    sems,
):
    pairs = (
        (flags_hbm, flags_ref),
        (yield_hbm, yield_ref),
        (state_hbm, state_ref),
        (density_hbm, density_ref),
    )
    copies = [
        pltpu.make_async_copy(source, target, sems.at[k])
        for k, (source, target) in enumerate(pairs)
    ]
    for copy in copies:
        copy.start()
    for copy in copies:
        copy.wait()
    odd = is_odd("depth")
    for (field, r), (width, at) in BESIDE.items():
        row = own_row(field, r - R, flags_ref, yield_ref, state_ref, density_ref)
        put_piece(row, width, at, odd, one_ref, two_ref)


def pack_corners(cut_one_ref, cut_two_ref, beside_one_ref, beside_two_ref, one_ref, two_ref):
    one_ref[:BESIDE_ROWS] = beside_one_ref[...]
    two_ref[:BESIDE_ROWS] = beside_two_ref[...]
    odd_cut, odd = is_odd("cut"), is_odd("depth")
    for (field, r), (width, at) in CORNERS.items():
        row = cut_row(field, r, odd_cut, cut_one_ref, cut_two_ref)
        put_piece(row, width, at, odd, one_ref, two_ref)


def steps_and_remap(
    place_ref,
    flags_ref,
    yield_ref,
    state_ref,
    density_ref,
    cut_one_ref,
    cut_two_ref,
    side_one_ref,
    side_two_ref,
    labels_ref,
    weights_ref,
    after_ref,
    outgoing_ref,
    tension,
    velocity,
    inverse,
    limits,
    rows,
    after,
    held,
    sems,
    after_sem,
):
    per = 2 * N

    def fetch(cx):
        return pltpu.make_async_copy(
            weights_ref.at[pl.ds(cx * per, per)], held.at[pl.ds(cx * per, per)], sems.at[cx]
        )

    for cx in range(N):
        fetch(cx).start()

    odd_cut, odd_depth = is_odd("cut"), is_odd("depth")
    for field in range(11):
        reach = REACH[field]
        for r in range(R - reach, R + N + reach):
            if R <= r < R + N:
                own = own_row(field, r - R, flags_ref, yield_ref, state_ref, density_ref)
            else:
                own = cut_row(field, r, odd_cut, cut_one_ref, cut_two_ref)
            width, at = PIECES.get((field, r), (0, 0))
            if width == 0:
                beside = [jnp.zeros((8, W), f32)]
            else:
                one, two = side_one_ref[at : at + width], side_two_ref[at : at + width]
                beside = [jnp.where(odd_depth, one, two), jnp.where(odd_depth, two, one)]
                if width < 4:
                    beside.insert(1, jnp.zeros((8 - 2 * width, W), f32))
            if field < 6:
                target = tension.at[field, r]
            elif field < 9:
                target = velocity.at[field - 6, r]
            else:
                target = (inverse if field == 9 else limits).at[r]
            target[:N] = own
            target[N:] = jnp.concatenate(beside, 0)

    def label(i, carry):
        for j in range(8):
            owner = i * 8 + j
            outgoing_ref[owner * TILES + CAP] = jnp.broadcast_to(labels_ref[owner], (8, W))
        return carry

    lax.fori_loop(0, DEV // 8, label, 0)

    lane = lax.broadcasted_iota(jnp.int32, (E, W), 1)
    first, last = lane == 0, lane == W - 1

    def along_depth(x):
        return pltpu.roll(x, E - 1, 0) - pltpu.roll(x, 1, 0)

    def along_width(x):
        up = jnp.where(last, 0.0, pltpu.roll(x, W - 1, 1))
        down = jnp.where(first, 0.0, pltpu.roll(x, 1, 1))
        return up - down

    def new_velocity(r):
        def along_cut(field):
            return tension[field, r + 1] - tension[field, r - 1]

        scale = inverse[r]
        xy, yz, xz = tension[3, r], tension[4, r], tension[5, r]
        return (
            velocity[0, r] + (along_cut(0) + along_depth(xy) + along_width(xz)) * scale,
            velocity[1, r] + (along_cut(3) + along_depth(tension[1, r]) + along_width(yz)) * scale,
            velocity[2, r] + (along_cut(5) + along_depth(yz) + along_width(tension[2, r])) * scale,
        )

    def new_stress(r):
        vx, vy, vz = velocity[0, r], velocity[1, r], velocity[2, r]
        limit = limits[r]

        def along_cut(field):
            return velocity[field, r + 1] - velocity[field, r - 1]

        xx, yy, zz = along_cut(0), along_depth(vy), along_width(vz)
        bulk = 0.075 * (xx + yy + zz)
        sxx = tension[0, r] + (0.09 * xx + bulk)
        syy = tension[1, r] + (0.09 * yy + bulk)
        szz = tension[2, r] + (0.09 * zz + bulk)
        sxy = tension[3, r] + 0.045 * (along_depth(vx) + along_cut(1))
        syz = tension[4, r] + 0.045 * (along_width(vy) + along_depth(vz))
        sxz = tension[5, r] + 0.045 * (along_width(vx) + along_cut(2))
        p = (sxx + syy + szz) * (1.0 / 3.0)
        dxx, dyy, dzz = sxx - p, syy - p, szz - p
        square = 1.5 * (
            dxx * dxx + dyy * dyy + dzz * dzz + 2.0 * (sxy * sxy + syz * syz + sxz * sxz)
        )
        factor = jnp.minimum(1.0, limit * lax.rsqrt(square))
        inside = limit > 0.0
        new = (
            p + factor * dxx,
            p + factor * dyy,
            p + factor * dzz,
            factor * sxy,
            factor * syz,
            factor * sxz,
        )
        return [jnp.where(inside, x, 0.0) for x in new]

    def sweep(start, stop, update, target):
        def body(i, carry):
            at = [start + GROUP * i + j for j in range(GROUP)]
            results = [update(r) for r in at]
            for r, result in zip(at, results):
                for field, x in enumerate(result):
                    target[field, r] = x
            return carry

        whole = (stop - start) // GROUP
        lax.fori_loop(0, whole, body, 0)
        rest = range(start + whole * GROUP, stop)
        for r, result in zip(rest, [update(r) for r in rest]):
            for field, x in enumerate(result):
                target[field, r] = x

    sweep(1, 23, new_velocity, velocity)
    sweep(2, 22, new_stress, tension)
    sweep(3, 21, new_velocity, velocity)

    def finish(i, carry):
        at = [GROUP * i + j for j in range(GROUP)]
        results = [new_stress(cx + R) for cx in at]
        for cx, result in zip(at, results):
            fields = [velocity[f, cx + R] for f in range(3)] + result
            for field, x in enumerate(fields):
                own = x[:N]
                after[field, cx] = own
                rows[cx, pl.ds(field, N, stride=16)] = own
        return carry

    lax.fori_loop(0, N // GROUP, finish, 0)
    keep = pltpu.make_async_copy(after, after_ref, after_sem)
    keep.start()

    def remap(cx, carry):
        fetch(cx).wait()
        for cy in range(0, N, 2):
            one = rows[cx, cy * 16 : (cy + 1) * 16].astype(jnp.bfloat16)
            two = rows[cx, (cy + 1) * 16 : (cy + 2) * 16].astype(jnp.bfloat16)
            none = jnp.zeros((16, W), jnp.bfloat16)
            blocks = jnp.concatenate(
                [jnp.concatenate([one, none], 1), jnp.concatenate([none, two], 1)], 0
            )
            pair = cx * per + 2 * cy
            spread = jnp.concatenate(
                [
                    jnp.concatenate([held[pair], held[pair + 1]], 1),
                    jnp.concatenate([held[pair + 2], held[pair + 3]], 1),
                ],
                0,
            )
            result = jnp.dot(blocks, spread, preferred_element_type=f32)
            for k in range(4):
                place = place_ref[pair + k]
                base = (place >> 3) * TILES
                rank = place & 7
                part = result[16 * (k // 2) : 16 * (k // 2) + 9, W * (k % 2) : W * (k % 2 + 1)]
                outgoing_ref[base + rank] = part[:8]
                outgoing_ref[base + CAP, pl.ds(rank, 1)] = part[8:9]
        return carry

    lax.fori_loop(0, N, remap, 0)
    keep.wait()


GROUP = 4
PARTS = 6
ROOM = SLOTS + 8


def gather(arrived, out_ref, turned, slots, sem, *sums):
    main, rest = sums[:PARTS], sums[PARTS:]
    named = arrived[:, CAP, CAP, :].T[:8].astype(jnp.int32)
    turned[...] = jnp.where(named == 0, SLOTS, named - 1)
    copy = pltpu.make_async_copy(turned, slots, sem)
    copy.start()
    for k in range(PARTS):
        main[k][...] = jnp.zeros((8 * ROOM, W), f32)
        rest[k][...] = jnp.zeros((ROOM, W), f32)
    copy.wait()

    def sources(i, carry):
        for j in range(UNROLL):
            source = i * UNROLL + j
            for k in range(CAP):
                slot = slots[k, source]
                tile = pl.ds(pl.multiple_of(slot * 8, 8), 8)
                main[k][tile] += arrived[source, k]
                rest[k][pl.ds(slot, 1)] += arrived[source, CAP, k : k + 1]
        return carry

    lax.fori_loop(0, DEV // UNROLL, sources, 0)

    def total(parts, spot):
        one, two, three = (parts[k][spot] + parts[k + 3][spot] for k in range(3))
        return one + two + three

    def fold(i, carry):
        spot = pl.ds(pl.multiple_of(i * W, W), W)
        main[0][spot] = total(main, spot)
        return carry

    lax.fori_loop(0, 8 * SLOTS // W, fold, 0)
    for field in range(8):
        out_ref[field] = main[0][pl.ds(field, SLOTS, stride=8)]
    out_ref[8] = total(rest, pl.ds(0, SLOTS))


UNROLL = 4


def exchange(one, two, axis):
    count = lax.axis_size(axis)

    def swap(first):
        pairs = [(i, i + 1) for i in range(first, count - 1, 2)]
        return pairs + [(high, low) for low, high in pairs]

    return lax.ppermute(one, axis, swap(1)), lax.ppermute(two, axis, swap(0))


VM = pl.BlockSpec(memory_space=pltpu.VMEM)
SM = pl.BlockSpec(memory_space=pltpu.SMEM)
HB = pl.BlockSpec(memory_space=pltpu.HBM)
SMALL = pltpu.CompilerParams(vmem_limit_bytes=8 * MIB)


def stay(x):
    return pltpu.with_memory_space_constraint(x, pltpu.HBM)


def both(rows):
    return (jax.ShapeDtypeStruct(rows + (W,), f32),) * 2


def on_device(
    initial_state, density, yield_flags, yield_stress, crossing_weights, new_owner, new_slot
):
    given = [stay(x) for x in (yield_flags, yield_stress, initial_state, density)]
    one, two = pl.pallas_call(
        pack_cut,
        out_shape=both((SLABS, N)),
        in_specs=[HB] * 4,
        out_specs=(VM, VM),
        scratch_shapes=[
            pltpu.VMEM((N, N), jnp.int32),
            pltpu.VMEM((N, N), f32),
            pltpu.VMEM((2, 3, N, W), f32),
            pltpu.SemaphoreType.DMA((22,)),
        ],
        compiler_params=SMALL,
        name="pack_cut",
    )(*given)
    cut_one, cut_two = exchange(one, two, "cut")
    beside_one, beside_two = pl.pallas_call(
        pack_beside,
        out_shape=both((BESIDE_ROWS,)),
        in_specs=[HB] * 4,
        out_specs=(VM, VM),
        scratch_shapes=[
            pltpu.VMEM((N, N), jnp.int32),
            pltpu.VMEM((N, N), f32),
            pltpu.VMEM((9, N, N, W), f32),
            pltpu.VMEM((N, N, W), f32),
            pltpu.SemaphoreType.DMA((4,)),
        ],
        compiler_params=SMALL,
        name="pack_beside",
    )(*given)
    one, two = pl.pallas_call(
        pack_corners,
        out_shape=both((SIDE_ROWS,)),
        in_specs=[VM] * 4,
        out_specs=(VM, VM),
        compiler_params=SMALL,
        name="pack_corners",
    )(cut_one, cut_two, beside_one, beside_two)
    side_one, side_two = exchange(one, two, "depth")

    owners = new_owner[:, 0]
    hits = (owners[:, None] == jnp.arange(DEV, dtype=jnp.int32)[None, :]).astype(jnp.int32)
    rank = jnp.sum((jnp.cumsum(hits, 0) - hits) * hits, 1)
    place = owners * 8 + rank
    by_rank = jnp.where(
        rank[:, None] == jnp.arange(W, dtype=jnp.int32)[None, :], new_slot[:, None] + 1, 0
    )
    labels = lax.dot_general(
        hits.astype(jnp.bfloat16),
        by_rank.astype(jnp.bfloat16),
        (((0,), (0,)), ((), ())),
        preferred_element_type=f32,
    )

    state_after, outgoing = pl.pallas_call(
        steps_and_remap,
        out_shape=(
            jax.ShapeDtypeStruct((9, N, N, W), f32),
            jax.ShapeDtypeStruct((DEV * TILES, 8, W), f32),
        ),
        in_specs=[SM] + [VM] * 9 + [HB],
        out_specs=(HB, VM),
        scratch_shapes=[
            pltpu.VMEM((6, E, E, W), f32),
            pltpu.VMEM((3, E, E, W), f32),
            pltpu.VMEM((E, E, W), f32),
            pltpu.VMEM((E, E, W), f32),
            pltpu.VMEM((N, N * 16, W), f32),
            pltpu.VMEM((9, N, N, W), f32),
            pltpu.VMEM((2 * N * N, W, W), jnp.bfloat16),
            pltpu.SemaphoreType.DMA((N,)),
            pltpu.SemaphoreType.DMA,
        ],
        compiler_params=pltpu.CompilerParams(vmem_limit_bytes=40 * MIB),
        name="steps_and_remap",
    )(
        place,
        yield_flags,
        yield_stress,
        initial_state,
        density,
        cut_one,
        cut_two,
        side_one,
        side_two,
        labels[:, None, :],
        stay(crossing_weights),
    )
    arrived = lax.all_to_all(outgoing, ("cut", "depth"), split_axis=0, concat_axis=0, tiled=True)
    new_integrals = pl.pallas_call(
        gather,
        out_shape=jax.ShapeDtypeStruct((9, SLOTS, W), f32),
        in_specs=[VM],
        out_specs=VM,
        scratch_shapes=[
            pltpu.VMEM((8, W), jnp.int32),
            pltpu.SMEM((8, W), jnp.int32),
            pltpu.SemaphoreType.DMA,
        ]
        + [pltpu.VMEM((8 * ROOM, W), f32)] * PARTS
        + [pltpu.VMEM((ROOM, W), f32)] * PARTS,
        compiler_params=pltpu.CompilerParams(vmem_limit_bytes=24 * MIB),
        name="gather",
    )(arrived.reshape(DEV, TILES, 8, W))
    return (state_after, new_integrals.transpose(1, 0, 2))


def solution(mesh):
    return jax.shard_map(
        on_device,
        mesh=mesh,
        in_specs=(
            P(None, "cut", "depth", None),
            P("cut", "depth", None),
            P("cut", "depth"),
            P("cut", "depth"),
            P(("cut", "depth"), None, None),
            P(("cut", "depth"), None),
            P(("cut", "depth")),
        ),
        out_specs=(P(None, "cut", "depth", None), P(("cut", "depth"), None, None)),
        check_vma=False,
    )
```

```python
import jax
import jax.numpy as jnp
from jax import lax
from jax.experimental import pallas as pl
from jax.experimental.pallas import tpu as pltpu
from jax.sharding import PartitionSpec as P

f32 = jnp.float32
N = 16
R = 4
E = N + 2 * R
W = 128
DEV = 128
CAP = 6
TILES = CAP + 1
SLOTS = 256
BIG = 1e30
MIB = 1024 * 1024

REACH = (4, 3, 3, 4, 3, 4, 3, 3, 3, 3, 2)
STARTS = tuple(sum(REACH[:field]) for field in range(10))
LIMIT_SLAB = sum(REACH[:10])
SLABS = LIMIT_SLAB + 1
WIDTH = (3, 4, 3, 4, 4, 3, 3, 3, 3, 3, 2)
RADIUS = (4,) * 6 + (3,) * 4 + (2,)


def pieces(corners, at):
    found = {}
    for field in range(11):
        for r in range(E):
            beyond = max(R - r, r - (R + N - 1), 0)
            width = WIDTH[field] if beyond == 0 else RADIUS[field] - beyond
            if width > 0 and (beyond > 0) == corners:
                found[field, r] = (width, at)
                at += width
    return found, at


BESIDE, BESIDE_ROWS = pieces(False, 0)
CORNERS, PIECE_ROWS = pieces(True, BESIDE_ROWS)
PIECES = BESIDE | CORNERS
SIDE_ROWS = -(-PIECE_ROWS // 8) * 8


def is_odd(axis):
    return lax.rem(lax.axis_index(axis), 2) == 1


def limit_row(flags_ref, stress_ref, row):
    along = jnp.where(
        flags_ref[row : row + 1] == 1, stress_ref[row : row + 1], BIG
    )
    square = jnp.broadcast_to(along, (N, N))
    diagonal = lax.broadcasted_iota(jnp.int32, (N, N), 0) == lax.broadcasted_iota(
        jnp.int32, (N, N), 1
    )
    column = jnp.sum(jnp.where(diagonal, square, 0.0), axis=1, keepdims=True)
    return jnp.broadcast_to(column, (N, W))


def scaled_inverse(density):
    return 0.075 / density


def pack_cut(
    flags_hbm, stress_hbm, state_ref, density_ref, one_ref, two_ref, flags_ref, stress_ref, edges, sems
):
    odd = lax.rem(lax.axis_index("cut"), 2)
    tops = ((one_ref, odd), (two_ref, 1 - odd))
    copies = [
        pltpu.make_async_copy(flags_hbm, flags_ref, sems.at[20]),
        pltpu.make_async_copy(stress_hbm, stress_ref, sems.at[21]),
    ]
    for field in range(9):
        source = state_ref.at[3 + field if field < 6 else field - 6]
        reach, start = REACH[field], STARTS[field]
        for side, (target, top) in enumerate(tops):
            copies.append(
                pltpu.make_async_copy(
                    source.at[pl.ds(top * (N - reach), reach)],
                    target.at[pl.ds(start, reach)],
                    sems.at[2 * field + side],
                )
            )
    for side, (target, top) in enumerate(tops):
        copies.append(
            pltpu.make_async_copy(
                density_ref.at[pl.ds(top * (N - 3), 3)], edges.at[side], sems.at[18 + side]
            )
        )
    for copy in copies:
        copy.start()
    copies[0].wait()
    copies[1].wait()
    half = lax.broadcasted_iota(jnp.int32, (N, W), 1) < W // 2
    slabs = [
        jnp.where(
            half,
            limit_row(flags_ref, stress_ref, row),
            limit_row(flags_ref, stress_ref, row + 1),
        )
        for row in (0, N - 2)
    ]
    for target, top in tops:
        target[LIMIT_SLAB] = jnp.where(top == 1, slabs[1], slabs[0])
    for copy in copies[2:]:
        copy.wait()
    for side, (target, top) in enumerate(tops):
        for row in range(3):
            target[STARTS[9] + row] = scaled_inverse(edges[side, row])


def cut_row(field, r, odd, one_ref, two_ref):
    def came(slab):
        one, two = one_ref[slab], two_ref[slab]
        return jnp.where(odd, two, one) if r < R else jnp.where(odd, one, two)

    if field == 10:
        slab = came(LIMIT_SLAB)
        first = lax.broadcasted_iota(jnp.int32, (N, W), 1) < W // 2
        wanted = first if r in (R - 2, R + N) else ~first
        return jnp.where(wanted, slab, pltpu.roll(slab, W // 2, 1))
    return came(STARTS[field] + (r - (R - REACH[field]) if r < R else r - R - N))


def own_row(field, row, flags_ref, yield_ref, state_ref, density_ref):
    if field < 6:
        return state_ref[3 + field, row]
    if field < 9:
        return state_ref[field - 6, row]
    if field == 9:
        return scaled_inverse(density_ref[row])
    return limit_row(flags_ref, yield_ref, row)


def put_piece(row, width, at, odd, one_ref, two_ref):
    low, high = row[:width], row[N - width :]
    one_ref[at : at + width] = jnp.where(odd, high, low)
    two_ref[at : at + width] = jnp.where(odd, low, high)


def pack_beside(
    flags_hbm,
    yield_hbm,
    state_hbm,
    density_hbm,
    one_ref,
    two_ref,
    flags_ref,
    yield_ref,
    state_ref,
    density_ref,
    sems,
):
    pairs = (
        (flags_hbm, flags_ref),
        (yield_hbm, yield_ref),
        (state_hbm, state_ref),
        (density_hbm, density_ref),
    )
    copies = [
        pltpu.make_async_copy(source, target, sems.at[k])
        for k, (source, target) in enumerate(pairs)
    ]
    for copy in copies:
        copy.start()
    for copy in copies:
        copy.wait()
    odd = is_odd("depth")
    for (field, r), (width, at) in BESIDE.items():
        row = own_row(field, r - R, flags_ref, yield_ref, state_ref, density_ref)
        put_piece(row, width, at, odd, one_ref, two_ref)


def pack_corners(cut_one_ref, cut_two_ref, beside_one_ref, beside_two_ref, one_ref, two_ref):
    one_ref[:BESIDE_ROWS] = beside_one_ref[...]
    two_ref[:BESIDE_ROWS] = beside_two_ref[...]
    odd_cut, odd = is_odd("cut"), is_odd("depth")
    for (field, r), (width, at) in CORNERS.items():
        row = cut_row(field, r, odd_cut, cut_one_ref, cut_two_ref)
        put_piece(row, width, at, odd, one_ref, two_ref)


def steps_and_remap(
    place_ref,
    flags_ref,
    yield_ref,
    state_ref,
    density_ref,
    cut_one_ref,
    cut_two_ref,
    side_one_ref,
    side_two_ref,
    labels_ref,
    ready_ref,
    weights_ref,
    after_ref,
    outgoing_ref,
    tension,
    velocity,
    inverse,
    limits,
    rows_even,
    rows_odd,
    after,
    held,
    sems,
    after_sem,
):
    per = 2 * N

    def fetch(cx):
        return pltpu.make_async_copy(
            weights_ref.at[pl.ds(cx * per, per)],
            held.at[pl.ds((cx - READY) * per, per)],
            sems.at[cx - READY],
        )

    for cx in range(READY, N):
        fetch(cx).start()

    odd_cut, odd_depth = is_odd("cut"), is_odd("depth")
    for field in range(11):
        reach = REACH[field]
        for r in range(R - reach, R + N + reach):
            if R <= r < R + N:
                own = own_row(field, r - R, flags_ref, yield_ref, state_ref, density_ref)
            else:
                own = cut_row(field, r, odd_cut, cut_one_ref, cut_two_ref)
            width, at = PIECES.get((field, r), (0, 0))
            if width == 0:
                beside = [jnp.zeros((8, W), f32)]
            else:
                one, two = side_one_ref[at : at + width], side_two_ref[at : at + width]
                beside = [jnp.where(odd_depth, one, two), jnp.where(odd_depth, two, one)]
                if width < 4:
                    beside.insert(1, jnp.zeros((8 - 2 * width, W), f32))
            if field < 6:
                target = tension.at[field, r]
            elif field < 9:
                target = velocity.at[field - 6, r]
            else:
                target = (inverse if field == 9 else limits).at[r]
            target[:N] = own
            target[N:] = jnp.concatenate(beside, 0)

    def label(i, carry):
        for j in range(8):
            owner = i * 8 + j
            outgoing_ref[owner * TILES + CAP] = jnp.broadcast_to(labels_ref[owner], (8, W))
        return carry

    lax.fori_loop(0, DEV // 8, label, 0)

    lane = lax.broadcasted_iota(jnp.int32, (E, W), 1)
    first, last = lane == 0, lane == W - 1

    def along_depth(x):
        return pltpu.roll(x, E - 1, 0) - pltpu.roll(x, 1, 0)

    def along_width(x):
        up = jnp.where(last, 0.0, pltpu.roll(x, W - 1, 1))
        down = jnp.where(first, 0.0, pltpu.roll(x, 1, 1))
        return up - down

    def new_velocity(r):
        def along_cut(field):
            return tension[field, r + 1] - tension[field, r - 1]

        scale = inverse[r]
        xy, yz, xz = tension[3, r], tension[4, r], tension[5, r]
        return (
            velocity[0, r] + (along_cut(0) + along_depth(xy) + along_width(xz)) * scale,
            velocity[1, r] + (along_cut(3) + along_depth(tension[1, r]) + along_width(yz)) * scale,
            velocity[2, r] + (along_cut(5) + along_depth(yz) + along_width(tension[2, r])) * scale,
        )

    def new_stress(r):
        vx, vy, vz = velocity[0, r], velocity[1, r], velocity[2, r]
        limit = limits[r]

        def along_cut(field):
            return velocity[field, r + 1] - velocity[field, r - 1]

        xx, yy, zz = along_cut(0), along_depth(vy), along_width(vz)
        bulk = 0.075 * (xx + yy + zz)
        sxx = tension[0, r] + (0.09 * xx + bulk)
        syy = tension[1, r] + (0.09 * yy + bulk)
        szz = tension[2, r] + (0.09 * zz + bulk)
        sxy = tension[3, r] + 0.045 * (along_depth(vx) + along_cut(1))
        syz = tension[4, r] + 0.045 * (along_width(vy) + along_depth(vz))
        sxz = tension[5, r] + 0.045 * (along_width(vx) + along_cut(2))
        p = (sxx + syy + szz) * (1.0 / 3.0)
        dxx, dyy, dzz = sxx - p, syy - p, szz - p
        square = 1.5 * (
            dxx * dxx + dyy * dyy + dzz * dzz + 2.0 * (sxy * sxy + syz * syz + sxz * sxz)
        )
        factor = jnp.minimum(1.0, limit * lax.rsqrt(square))
        inside = limit > 0.0
        new = (
            p + factor * dxx,
            p + factor * dyy,
            p + factor * dzz,
            factor * sxy,
            factor * syz,
            factor * sxz,
        )
        return [jnp.where(inside, x, 0.0) for x in new]

    def sweep(start, stop, update, target):
        for low in range(start, stop, GROUP):
            at = range(low, min(low + GROUP, stop))
            for r, result in zip(at, [update(r) for r in at]):
                for field, x in enumerate(result):
                    target[field, r] = x

    def finish(i, target):
        at = range(BATCH * i, BATCH * (i + 1))
        results = [new_stress(cx + R) for cx in at]
        for j, (cx, result) in enumerate(zip(at, results)):
            fields = [velocity[f, cx + R] for f in range(3)] + result
            for field, x in enumerate(fields):
                own = x[:N]
                after[field, cx] = own
                target[j, pl.ds(field, N, stride=16)] = own

    def remap(i, source):
        none = jnp.zeros((16, W), jnp.bfloat16)
        for j in range(BATCH):
            for cy in range(0, N, 2):
                one = source[j, cy * 16 : (cy + 1) * 16].astype(jnp.bfloat16)
                two = source[j, (cy + 1) * 16 : (cy + 2) * 16].astype(jnp.bfloat16)
                blocks = jnp.concatenate(
                    [jnp.concatenate([one, none], 1), jnp.concatenate([none, two], 1)], 0
                )
                pair = (BATCH * i + j) * per + 2 * cy
                here, at = (ready_ref, pair) if BATCH * i < READY else (held, pair - READY * per)
                spread = jnp.concatenate(
                    [
                        jnp.concatenate([here[at], here[at + 1]], 1),
                        jnp.concatenate([here[at + 2], here[at + 3]], 1),
                    ],
                    0,
                )
                result = jnp.dot(blocks, spread, preferred_element_type=f32)
                for k in range(4):
                    place = place_ref[pair + k]
                    base = (place >> 3) * TILES
                    rank = place & 7
                    row, column = 16 * (k // 2), W * (k % 2)
                    part = result[row : row + 9, column : column + W]
                    outgoing_ref[base + rank] = part[:8]
                    outgoing_ref[base + CAP, pl.ds(rank, 1)] = part[8:9]

    keep = pltpu.make_async_copy(after, after_ref, after_sem)
    batches = N // BATCH
    for i in range(batches + 1):
        for cx in range(max(READY, BATCH * (i - 1)), BATCH * i):
            fetch(cx).wait()
        if i < batches:
            end = R + BATCH * (i + 1)
            sweep(end - BATCH + 3 if i else 1, end + 3, new_velocity, velocity)
            sweep(end - BATCH + 2 if i else 2, end + 2, new_stress, tension)
            sweep(end - BATCH + 1 if i else 3, end + 1, new_velocity, velocity)
            finish(i, (rows_even, rows_odd)[i % 2])
        if i == batches - 1:
            keep.start()
        if i > 0:
            remap(i - 1, (rows_even, rows_odd)[(i - 1) % 2])
    keep.wait()


BATCH = 4
READY = 8
GROUP = 4
PARTS = 3
ROOM = SLOTS + 8


def gather(arrived, out_ref, turned, slots, sem, *sums):
    main, rest = sums[:PARTS], sums[PARTS:]
    named = arrived[:, CAP, CAP, :].T[:8].astype(jnp.int32)
    turned[...] = jnp.where(named == 0, SLOTS, named - 1)
    copy = pltpu.make_async_copy(turned, slots, sem)
    copy.start()
    for k in range(PARTS):
        main[k][...] = jnp.zeros((8 * ROOM, W), f32)
        rest[k][...] = jnp.zeros((ROOM, W), f32)
    copy.wait()

    def sources(i, carry):
        for j in range(UNROLL):
            source = i * UNROLL + j
            for k in range(CAP):
                part = k % PARTS
                slot = slots[k, source]
                tile = pl.ds(pl.multiple_of(slot * 8, 8), 8)
                main[part][tile] += arrived[source, k]
                rest[part][pl.ds(slot, 1)] += arrived[source, CAP, k : k + 1]
        return carry

    lax.fori_loop(0, DEV // UNROLL, sources, 0)

    def total(parts, spot):
        return parts[0][spot] + parts[1][spot] + parts[2][spot]

    def fold(i, carry):
        spot = pl.ds(pl.multiple_of(i * W, W), W)
        main[0][spot] = total(main, spot)
        return carry

    lax.fori_loop(0, 8 * SLOTS // W, fold, 0)
    for field in range(8):
        out_ref[field] = main[0][pl.ds(field, SLOTS, stride=8)]
    out_ref[8] = total(rest, pl.ds(0, SLOTS))


UNROLL = 4


def bring(weights_ref, ready_ref, sems):
    part = READY * 2 * N // 8
    copies = [
        pltpu.make_async_copy(
            weights_ref.at[pl.ds(k * part, part)], ready_ref.at[pl.ds(k * part, part)], sems.at[k]
        )
        for k in range(8)
    ]
    for copy in copies:
        copy.start()
    for copy in copies:
        copy.wait()


def exchange(one, two, axis):
    count = lax.axis_size(axis)

    def swap(first):
        pairs = [(i, i + 1) for i in range(first, count - 1, 2)]
        return pairs + [(high, low) for low, high in pairs]

    return lax.ppermute(one, axis, swap(1)), lax.ppermute(two, axis, swap(0))


VM = pl.BlockSpec(memory_space=pltpu.VMEM)
SM = pl.BlockSpec(memory_space=pltpu.SMEM)
HB = pl.BlockSpec(memory_space=pltpu.HBM)
SMALL = pltpu.CompilerParams(vmem_limit_bytes=8 * MIB)


def stay(x):
    return pltpu.with_memory_space_constraint(x, pltpu.HBM)


def both(rows):
    return (jax.ShapeDtypeStruct(rows + (W,), f32),) * 2


def on_device(
    initial_state, density, yield_flags, yield_stress, crossing_weights, new_owner, new_slot
):
    given = [stay(x) for x in (yield_flags, yield_stress, initial_state, density)]
    one, two = pl.pallas_call(
        pack_cut,
        out_shape=both((SLABS, N)),
        in_specs=[HB] * 4,
        out_specs=(VM, VM),
        scratch_shapes=[
            pltpu.VMEM((N, N), jnp.int32),
            pltpu.VMEM((N, N), f32),
            pltpu.VMEM((2, 3, N, W), f32),
            pltpu.SemaphoreType.DMA((22,)),
        ],
        compiler_params=SMALL,
        name="pack_cut",
    )(*given)
    cut_one, cut_two = exchange(one, two, "cut")
    beside_one, beside_two = pl.pallas_call(
        pack_beside,
        out_shape=both((BESIDE_ROWS,)),
        in_specs=[HB] * 4,
        out_specs=(VM, VM),
        scratch_shapes=[
            pltpu.VMEM((N, N), jnp.int32),
            pltpu.VMEM((N, N), f32),
            pltpu.VMEM((9, N, N, W), f32),
            pltpu.VMEM((N, N, W), f32),
            pltpu.SemaphoreType.DMA((4,)),
        ],
        compiler_params=SMALL,
        name="pack_beside",
    )(*given)
    one, two = pl.pallas_call(
        pack_corners,
        out_shape=both((SIDE_ROWS,)),
        in_specs=[VM] * 4,
        out_specs=(VM, VM),
        compiler_params=SMALL,
        name="pack_corners",
    )(cut_one, cut_two, beside_one, beside_two)
    one, two, weights = lax.optimization_barrier((one, two, crossing_weights))
    side_one, side_two = exchange(one, two, "depth")
    ready = pl.pallas_call(
        bring,
        out_shape=jax.ShapeDtypeStruct((READY * 2 * N, W, W), jnp.bfloat16),
        in_specs=[HB],
        out_specs=VM,
        scratch_shapes=[pltpu.SemaphoreType.DMA((8,))],
        compiler_params=pltpu.CompilerParams(vmem_limit_bytes=12 * MIB),
        cost_estimate=pl.CostEstimate(
            flops=0, bytes_accessed=READY * 2 * N * W * W * 2, transcendentals=0
        ),
        name="bring",
    )(stay(weights))

    owners = new_owner[:, 0]
    hits = (owners[:, None] == jnp.arange(DEV, dtype=jnp.int32)[None, :]).astype(jnp.int32)
    rank = jnp.sum((jnp.cumsum(hits, 0) - hits) * hits, 1)
    place = owners * 8 + rank
    by_rank = jnp.where(
        rank[:, None] == jnp.arange(W, dtype=jnp.int32)[None, :], new_slot[:, None] + 1, 0
    )
    labels = lax.dot_general(
        hits.astype(jnp.bfloat16),
        by_rank.astype(jnp.bfloat16),
        (((0,), (0,)), ((), ())),
        preferred_element_type=f32,
    )

    state_after, outgoing = pl.pallas_call(
        steps_and_remap,
        out_shape=(
            jax.ShapeDtypeStruct((9, N, N, W), f32),
            jax.ShapeDtypeStruct((DEV * TILES, 8, W), f32),
        ),
        in_specs=[SM] + [VM] * 10 + [HB],
        out_specs=(HB, VM),
        scratch_shapes=[
            pltpu.VMEM((6, E, E, W), f32),
            pltpu.VMEM((3, E, E, W), f32),
            pltpu.VMEM((E, E, W), f32),
            pltpu.VMEM((E, E, W), f32),
            pltpu.VMEM((BATCH, N * 16, W), f32),
            pltpu.VMEM((BATCH, N * 16, W), f32),
            pltpu.VMEM((9, N, N, W), f32),
            pltpu.VMEM(((N - READY) * 2 * N, W, W), jnp.bfloat16),
            pltpu.SemaphoreType.DMA((N - READY,)),
            pltpu.SemaphoreType.DMA,
        ],
        compiler_params=pltpu.CompilerParams(vmem_limit_bytes=24 * MIB),
        name="steps_and_remap",
    )(
        place,
        yield_flags,
        yield_stress,
        initial_state,
        density,
        cut_one,
        cut_two,
        side_one,
        side_two,
        labels[:, None, :],
        ready,
        stay(crossing_weights),
    )
    arrived = lax.all_to_all(outgoing, ("cut", "depth"), split_axis=0, concat_axis=0, tiled=True)
    new_integrals = pl.pallas_call(
        gather,
        out_shape=jax.ShapeDtypeStruct((9, SLOTS, W), f32),
        in_specs=[VM],
        out_specs=VM,
        scratch_shapes=[
            pltpu.VMEM((8, W), jnp.int32),
            pltpu.SMEM((8, W), jnp.int32),
            pltpu.SemaphoreType.DMA,
        ]
        + [pltpu.VMEM((8 * ROOM, W), f32)] * PARTS
        + [pltpu.VMEM((ROOM, W), f32)] * PARTS,
        compiler_params=pltpu.CompilerParams(vmem_limit_bytes=24 * MIB),
        name="gather",
    )(arrived.reshape(DEV, TILES, 8, W))
    return (state_after, new_integrals.transpose(1, 0, 2))


def solution(mesh):
    return jax.shard_map(
        on_device,
        mesh=mesh,
        in_specs=(
            P(None, "cut", "depth", None),
            P("cut", "depth", None),
            P("cut", "depth"),
            P("cut", "depth"),
            P(("cut", "depth"), None, None),
            P(("cut", "depth"), None),
            P(("cut", "depth")),
        ),
        out_specs=(P(None, "cut", "depth", None), P(("cut", "depth"), None, None)),
        check_vma=False,
    )
```

```python
import jax
import jax.numpy as jnp
from jax import lax
from jax.experimental import pallas as pl
from jax.experimental.pallas import tpu as pltpu
from jax.sharding import PartitionSpec as P

f32 = jnp.float32
N = 16
R = 4
E = N + 2 * R
W = 128
DEV = 128
CAP = 6
TILES = CAP + 1
SLOTS = 256
BIG = 1e30
MIB = 1024 * 1024

REACH = (4, 3, 3, 4, 3, 4, 3, 3, 3, 3, 2)
STARTS = tuple(sum(REACH[:field]) for field in range(10))
LIMIT_SLAB = sum(REACH[:10])
SLABS = LIMIT_SLAB + 1
WIDTH = (3, 4, 3, 4, 4, 3, 3, 3, 3, 3, 2)
RADIUS = (4,) * 6 + (3,) * 4 + (2,)


def pieces(corners, at):
    found = {}
    for field in range(11):
        for r in range(E):
            beyond = max(R - r, r - (R + N - 1), 0)
            width = WIDTH[field] if beyond == 0 else RADIUS[field] - beyond
            if width > 0 and (beyond > 0) == corners:
                found[field, r] = (width, at)
                at += width
    return found, at


BESIDE, BESIDE_ROWS = pieces(False, 0)
CORNERS, PIECE_ROWS = pieces(True, BESIDE_ROWS)
PIECES = BESIDE | CORNERS
SIDE_ROWS = -(-PIECE_ROWS // 8) * 8
CORNER_ROWS = SIDE_ROWS - BESIDE_ROWS


def is_odd(axis):
    return lax.rem(lax.axis_index(axis), 2) == 1


def limit_row(flags_ref, stress_ref, row):
    along = jnp.where(
        flags_ref[row : row + 1] == 1, stress_ref[row : row + 1], BIG
    )
    square = jnp.broadcast_to(along, (N, N))
    diagonal = lax.broadcasted_iota(jnp.int32, (N, N), 0) == lax.broadcasted_iota(
        jnp.int32, (N, N), 1
    )
    column = jnp.sum(jnp.where(diagonal, square, 0.0), axis=1, keepdims=True)
    return jnp.broadcast_to(column, (N, W))


def scaled_inverse(density):
    return 0.075 / density


def pack_cut(
    flags_hbm, stress_hbm, state_ref, density_ref, one_ref, two_ref, flags_ref, stress_ref, edges, sems
):
    odd = lax.rem(lax.axis_index("cut"), 2)
    tops = ((one_ref, odd), (two_ref, 1 - odd))
    copies = [
        pltpu.make_async_copy(flags_hbm, flags_ref, sems.at[20]),
        pltpu.make_async_copy(stress_hbm, stress_ref, sems.at[21]),
    ]
    for field in range(9):
        source = state_ref.at[3 + field if field < 6 else field - 6]
        reach, start = REACH[field], STARTS[field]
        for side, (target, top) in enumerate(tops):
            copies.append(
                pltpu.make_async_copy(
                    source.at[pl.ds(top * (N - reach), reach)],
                    target.at[pl.ds(start, reach)],
                    sems.at[2 * field + side],
                )
            )
    for side, (target, top) in enumerate(tops):
        copies.append(
            pltpu.make_async_copy(
                density_ref.at[pl.ds(top * (N - 3), 3)], edges.at[side], sems.at[18 + side]
            )
        )
    for copy in copies:
        copy.start()
    copies[0].wait()
    copies[1].wait()
    half = lax.broadcasted_iota(jnp.int32, (N, W), 1) < W // 2
    slabs = [
        jnp.where(
            half,
            limit_row(flags_ref, stress_ref, row),
            limit_row(flags_ref, stress_ref, row + 1),
        )
        for row in (0, N - 2)
    ]
    for target, top in tops:
        target[LIMIT_SLAB] = jnp.where(top == 1, slabs[1], slabs[0])
    for copy in copies[2:]:
        copy.wait()
    for side, (target, top) in enumerate(tops):
        for row in range(3):
            target[STARTS[9] + row] = scaled_inverse(edges[side, row])


def cut_row(field, r, odd, one_ref, two_ref):
    def came(slab):
        one, two = one_ref[slab], two_ref[slab]
        return jnp.where(odd, two, one) if r < R else jnp.where(odd, one, two)

    if field == 10:
        slab = came(LIMIT_SLAB)
        first = lax.broadcasted_iota(jnp.int32, (N, W), 1) < W // 2
        wanted = first if r in (R - 2, R + N) else ~first
        return jnp.where(wanted, slab, pltpu.roll(slab, W // 2, 1))
    return came(STARTS[field] + (r - (R - REACH[field]) if r < R else r - R - N))


def own_row(field, row, flags_ref, yield_ref, state_ref, density_ref):
    if field < 6:
        return state_ref[3 + field, row]
    if field < 9:
        return state_ref[field - 6, row]
    if field == 9:
        return scaled_inverse(density_ref[row])
    return limit_row(flags_ref, yield_ref, row)


def put_piece(row, width, odd, one_ref, one_at, two_ref, two_at):
    low, high = row[:width], row[N - width :]
    one_ref[one_at : one_at + width] = jnp.where(odd, high, low)
    two_ref[two_at : two_at + width] = jnp.where(odd, low, high)


def pack_beside(
    flags_hbm,
    yield_hbm,
    state_hbm,
    density_hbm,
    one_ref,
    two_ref,
    flags_ref,
    yield_ref,
    state_ref,
    density_ref,
    sems,
):
    pairs = (
        (flags_hbm, flags_ref),
        (yield_hbm, yield_ref),
        (state_hbm, state_ref),
        (density_hbm, density_ref),
    )
    copies = [
        pltpu.make_async_copy(source, target, sems.at[k])
        for k, (source, target) in enumerate(pairs)
    ]
    for copy in copies:
        copy.start()
    for copy in copies:
        copy.wait()
    odd = is_odd("depth")
    for (field, r), (width, at) in BESIDE.items():
        row = own_row(field, r - R, flags_ref, yield_ref, state_ref, density_ref)
        put_piece(row, width, odd, one_ref, at, two_ref, at)


def pack_corners(cut_one_ref, cut_two_ref, beside_two_ref, one_ref, two_ref):
    two_ref[:BESIDE_ROWS] = beside_two_ref[...]
    odd_cut, odd = is_odd("cut"), is_odd("depth")
    for (field, r), (width, at) in CORNERS.items():
        row = cut_row(field, r, odd_cut, cut_one_ref, cut_two_ref)
        put_piece(row, width, odd, one_ref, at - BESIDE_ROWS, two_ref, at)


def steps_and_remap(
    place_ref,
    flags_ref,
    yield_ref,
    state_ref,
    density_ref,
    cut_one_ref,
    cut_two_ref,
    beside_one_ref,
    corner_one_ref,
    side_two_ref,
    labels_ref,
    ready_ref,
    weights_ref,
    after_ref,
    outgoing_ref,
    tension,
    velocity,
    inverse,
    limits,
    rows_even,
    rows_odd,
    after,
    held,
    sems,
    after_sem,
):
    per = 2 * N

    def fetch(cx):
        return pltpu.make_async_copy(
            weights_ref.at[pl.ds(cx * per, per)],
            held.at[pl.ds((cx - READY) * per, per)],
            sems.at[cx - READY],
        )

    for cx in range(READY, N):
        fetch(cx).start()

    odd_cut, odd_depth = is_odd("cut"), is_odd("depth")
    for field in range(11):
        reach = REACH[field]
        for r in range(R - reach, R + N + reach):
            if R <= r < R + N:
                own = own_row(field, r - R, flags_ref, yield_ref, state_ref, density_ref)
            else:
                own = cut_row(field, r, odd_cut, cut_one_ref, cut_two_ref)
            width, at = PIECES.get((field, r), (0, 0))
            if width == 0:
                beside = [jnp.zeros((8, W), f32)]
            else:
                two = side_two_ref[at : at + width]
                if at < BESIDE_ROWS:
                    one = beside_one_ref[at : at + width]
                else:
                    one = corner_one_ref[at - BESIDE_ROWS : at - BESIDE_ROWS + width]
                beside = [jnp.where(odd_depth, one, two), jnp.where(odd_depth, two, one)]
                if width < 4:
                    beside.insert(1, jnp.zeros((8 - 2 * width, W), f32))
            if field < 6:
                target = tension.at[field, r]
            elif field < 9:
                target = velocity.at[field - 6, r]
            else:
                target = (inverse if field == 9 else limits).at[r]
            target[:N] = own
            target[N:] = jnp.concatenate(beside, 0)

    def label(i, carry):
        for j in range(8):
            owner = i * 8 + j
            outgoing_ref[owner * TILES + CAP] = jnp.broadcast_to(labels_ref[owner], (8, W))
        return carry

    lax.fori_loop(0, DEV // 8, label, 0)

    lane = lax.broadcasted_iota(jnp.int32, (E, W), 1)
    first, last = lane == 0, lane == W - 1

    def along_depth(x):
        return pltpu.roll(x, E - 1, 0) - pltpu.roll(x, 1, 0)

    def along_width(x):
        up = jnp.where(last, 0.0, pltpu.roll(x, W - 1, 1))
        down = jnp.where(first, 0.0, pltpu.roll(x, 1, 1))
        return up - down

    def new_velocity(r):
        def along_cut(field):
            return tension[field, r + 1] - tension[field, r - 1]

        scale = inverse[r]
        xy, yz, xz = tension[3, r], tension[4, r], tension[5, r]
        return (
            velocity[0, r] + (along_cut(0) + along_depth(xy) + along_width(xz)) * scale,
            velocity[1, r] + (along_cut(3) + along_depth(tension[1, r]) + along_width(yz)) * scale,
            velocity[2, r] + (along_cut(5) + along_depth(yz) + along_width(tension[2, r])) * scale,
        )

    def new_stress(r):
        vx, vy, vz = velocity[0, r], velocity[1, r], velocity[2, r]
        limit = limits[r]

        def along_cut(field):
            return velocity[field, r + 1] - velocity[field, r - 1]

        xx, yy, zz = along_cut(0), along_depth(vy), along_width(vz)
        bulk = 0.075 * (xx + yy + zz)
        sxx = tension[0, r] + (0.09 * xx + bulk)
        syy = tension[1, r] + (0.09 * yy + bulk)
        szz = tension[2, r] + (0.09 * zz + bulk)
        sxy = tension[3, r] + 0.045 * (along_depth(vx) + along_cut(1))
        syz = tension[4, r] + 0.045 * (along_width(vy) + along_depth(vz))
        sxz = tension[5, r] + 0.045 * (along_width(vx) + along_cut(2))
        p = (sxx + syy + szz) * (1.0 / 3.0)
        dxx, dyy, dzz = sxx - p, syy - p, szz - p
        square = 1.5 * (
            dxx * dxx + dyy * dyy + dzz * dzz + 2.0 * (sxy * sxy + syz * syz + sxz * sxz)
        )
        factor = jnp.minimum(1.0, limit * lax.rsqrt(square))
        inside = limit > 0.0
        new = (
            p + factor * dxx,
            p + factor * dyy,
            p + factor * dzz,
            factor * sxy,
            factor * syz,
            factor * sxz,
        )
        return [jnp.where(inside, x, 0.0) for x in new]

    def sweep(start, stop, update, target):
        for low in range(start, stop, GROUP):
            at = range(low, min(low + GROUP, stop))
            for r, result in zip(at, [update(r) for r in at]):
                for field, x in enumerate(result):
                    target[field, r] = x

    def finish(i, target):
        at = range(BATCH * i, BATCH * (i + 1))
        results = [new_stress(cx + R) for cx in at]
        for j, (cx, result) in enumerate(zip(at, results)):
            fields = [velocity[f, cx + R] for f in range(3)] + result
            for field, x in enumerate(fields):
                own = x[:N]
                after[field, cx] = own
                target[j, pl.ds(field, N, stride=16)] = own

    def remap(i, source):
        none = jnp.zeros((16, W), jnp.bfloat16)
        for j in range(BATCH):
            for cy in range(0, N, 2):
                one = source[j, cy * 16 : (cy + 1) * 16].astype(jnp.bfloat16)
                two = source[j, (cy + 1) * 16 : (cy + 2) * 16].astype(jnp.bfloat16)
                blocks = jnp.concatenate(
                    [jnp.concatenate([one, none], 1), jnp.concatenate([none, two], 1)], 0
                )
                pair = (BATCH * i + j) * per + 2 * cy
                here, at = (ready_ref, pair) if BATCH * i < READY else (held, pair - READY * per)
                spread = jnp.concatenate(
                    [
                        jnp.concatenate([here[at], here[at + 1]], 1),
                        jnp.concatenate([here[at + 2], here[at + 3]], 1),
                    ],
                    0,
                )
                result = jnp.dot(blocks, spread, preferred_element_type=f32)
                for k in range(4):
                    place = place_ref[pair + k]
                    base = (place >> 3) * TILES
                    rank = place & 7
                    row, column = 16 * (k // 2), W * (k % 2)
                    part = result[row : row + 9, column : column + W]
                    outgoing_ref[base + rank] = part[:8]
                    outgoing_ref[base + CAP, pl.ds(rank, 1)] = part[8:9]

    keep = pltpu.make_async_copy(after, after_ref, after_sem)
    batches = N // BATCH
    for i in range(batches + 1):
        for cx in range(max(READY, BATCH * (i - 1)), BATCH * i):
            fetch(cx).wait()
        if i < batches:
            end = R + BATCH * (i + 1)
            sweep(end - BATCH + 3 if i else 1, end + 3, new_velocity, velocity)
            sweep(end - BATCH + 2 if i else 2, end + 2, new_stress, tension)
            sweep(end - BATCH + 1 if i else 3, end + 1, new_velocity, velocity)
            finish(i, (rows_even, rows_odd)[i % 2])
        if i == batches - 1:
            keep.start()
        if i > 0:
            remap(i - 1, (rows_even, rows_odd)[(i - 1) % 2])
    keep.wait()


BATCH = 4
READY = 4
GROUP = 4
PARTS = 3
ROOM = SLOTS + 8


def gather(arrived, out_ref, turned, slots, sem, *sums):
    main, rest = sums[:PARTS], sums[PARTS:]
    named = arrived[:, CAP, CAP, :].T[:8].astype(jnp.int32)
    turned[...] = jnp.where(named == 0, SLOTS, named - 1)
    copy = pltpu.make_async_copy(turned, slots, sem)
    copy.start()
    for k in range(PARTS):
        main[k][...] = jnp.zeros((8 * ROOM, W), f32)
        rest[k][...] = jnp.zeros((ROOM, W), f32)
    copy.wait()

    def sources(i, carry):
        for j in range(UNROLL):
            source = i * UNROLL + j
            for k in range(CAP):
                part = k % PARTS
                slot = slots[k, source]
                tile = pl.ds(pl.multiple_of(slot * 8, 8), 8)
                main[part][tile] += arrived[source, k]
                rest[part][pl.ds(slot, 1)] += arrived[source, CAP, k : k + 1]
        return carry

    lax.fori_loop(0, DEV // UNROLL, sources, 0)

    def total(parts, spot):
        return parts[0][spot] + parts[1][spot] + parts[2][spot]

    def fold(i, carry):
        spot = pl.ds(pl.multiple_of(i * W, W), W)
        main[0][spot] = total(main, spot)
        return carry

    lax.fori_loop(0, 8 * SLOTS // W, fold, 0)
    for field in range(8):
        out_ref[field] = main[0][pl.ds(field, SLOTS, stride=8)]
    out_ref[8] = total(rest, pl.ds(0, SLOTS))


UNROLL = 4


def bring(weights_ref, ready_ref, sems):
    part = READY * 2 * N // 8
    copies = [
        pltpu.make_async_copy(
            weights_ref.at[pl.ds(k * part, part)], ready_ref.at[pl.ds(k * part, part)], sems.at[k]
        )
        for k in range(8)
    ]
    for copy in copies:
        copy.start()
    for copy in copies:
        copy.wait()


def exchange(x, axis, first):
    pairs = [(i, i + 1) for i in range(first, lax.axis_size(axis) - 1, 2)]
    return lax.ppermute(x, axis, pairs + [(high, low) for low, high in pairs])


VM = pl.BlockSpec(memory_space=pltpu.VMEM)
SM = pl.BlockSpec(memory_space=pltpu.SMEM)
HB = pl.BlockSpec(memory_space=pltpu.HBM)
SMALL = pltpu.CompilerParams(vmem_limit_bytes=8 * MIB)


def stay(x):
    return pltpu.with_memory_space_constraint(x, pltpu.HBM)


def both(rows):
    return (jax.ShapeDtypeStruct(rows + (W,), f32),) * 2


def on_device(
    initial_state, density, yield_flags, yield_stress, crossing_weights, new_owner, new_slot
):
    given = [stay(x) for x in (yield_flags, yield_stress, initial_state, density)]
    one, two = pl.pallas_call(
        pack_cut,
        out_shape=both((SLABS, N)),
        in_specs=[HB] * 4,
        out_specs=(VM, VM),
        scratch_shapes=[
            pltpu.VMEM((N, N), jnp.int32),
            pltpu.VMEM((N, N), f32),
            pltpu.VMEM((2, 3, N, W), f32),
            pltpu.SemaphoreType.DMA((22,)),
        ],
        compiler_params=SMALL,
        name="pack_cut",
    )(*given)
    cut_one, cut_two = exchange(one, "cut", 1), exchange(two, "cut", 0)
    beside_one, beside_two = pl.pallas_call(
        pack_beside,
        out_shape=both((BESIDE_ROWS,)),
        in_specs=[HB] * 4,
        out_specs=(VM, VM),
        scratch_shapes=[
            pltpu.VMEM((N, N), jnp.int32),
            pltpu.VMEM((N, N), f32),
            pltpu.VMEM((9, N, N, W), f32),
            pltpu.VMEM((N, N, W), f32),
            pltpu.SemaphoreType.DMA((4,)),
        ],
        compiler_params=SMALL,
        name="pack_beside",
    )(*given)
    beside_one, beside_two, weights = lax.optimization_barrier(
        (beside_one, beside_two, crossing_weights)
    )
    beside_one = exchange(beside_one, "depth", 1)
    one, two = pl.pallas_call(
        pack_corners,
        out_shape=both((CORNER_ROWS,))[:1] + both((SIDE_ROWS,))[:1],
        in_specs=[VM] * 3,
        out_specs=(VM, VM),
        compiler_params=SMALL,
        name="pack_corners",
    )(cut_one, cut_two, beside_two)
    corner_one, side_two = exchange(one, "depth", 1), exchange(two, "depth", 0)
    ready = pl.pallas_call(
        bring,
        out_shape=jax.ShapeDtypeStruct((READY * 2 * N, W, W), jnp.bfloat16),
        in_specs=[HB],
        out_specs=VM,
        scratch_shapes=[pltpu.SemaphoreType.DMA((8,))],
        compiler_params=pltpu.CompilerParams(vmem_limit_bytes=12 * MIB),
        cost_estimate=pl.CostEstimate(
            flops=0, bytes_accessed=READY * 2 * N * W * W * 2, transcendentals=0
        ),
        name="bring",
    )(stay(weights))

    owners = new_owner[:, 0]
    hits = (owners[:, None] == jnp.arange(DEV, dtype=jnp.int32)[None, :]).astype(jnp.int32)
    rank = jnp.sum((jnp.cumsum(hits, 0) - hits) * hits, 1)
    place = owners * 8 + rank
    by_rank = jnp.where(
        rank[:, None] == jnp.arange(W, dtype=jnp.int32)[None, :], new_slot[:, None] + 1, 0
    )
    labels = lax.dot_general(
        hits.astype(jnp.bfloat16),
        by_rank.astype(jnp.bfloat16),
        (((0,), (0,)), ((), ())),
        preferred_element_type=f32,
    )

    state_after, outgoing = pl.pallas_call(
        steps_and_remap,
        out_shape=(
            jax.ShapeDtypeStruct((9, N, N, W), f32),
            jax.ShapeDtypeStruct((DEV * TILES, 8, W), f32),
        ),
        in_specs=[SM] + [VM] * 11 + [HB],
        out_specs=(HB, VM),
        scratch_shapes=[
            pltpu.VMEM((6, E, E, W), f32),
            pltpu.VMEM((3, E, E, W), f32),
            pltpu.VMEM((E, E, W), f32),
            pltpu.VMEM((E, E, W), f32),
            pltpu.VMEM((BATCH, N * 16, W), f32),
            pltpu.VMEM((BATCH, N * 16, W), f32),
            pltpu.VMEM((9, N, N, W), f32),
            pltpu.VMEM(((N - READY) * 2 * N, W, W), jnp.bfloat16),
            pltpu.SemaphoreType.DMA((N - READY,)),
            pltpu.SemaphoreType.DMA,
        ],
        compiler_params=pltpu.CompilerParams(vmem_limit_bytes=24 * MIB),
        name="steps_and_remap",
    )(
        place,
        yield_flags,
        yield_stress,
        initial_state,
        density,
        cut_one,
        cut_two,
        beside_one,
        corner_one,
        side_two,
        labels[:, None, :],
        ready,
        stay(crossing_weights),
    )
    arrived = lax.all_to_all(outgoing, ("cut", "depth"), split_axis=0, concat_axis=0, tiled=True)
    new_integrals = pl.pallas_call(
        gather,
        out_shape=jax.ShapeDtypeStruct((9, SLOTS, W), f32),
        in_specs=[VM],
        out_specs=VM,
        scratch_shapes=[
            pltpu.VMEM((8, W), jnp.int32),
            pltpu.SMEM((8, W), jnp.int32),
            pltpu.SemaphoreType.DMA,
        ]
        + [pltpu.VMEM((8 * ROOM, W), f32)] * PARTS
        + [pltpu.VMEM((ROOM, W), f32)] * PARTS,
        compiler_params=pltpu.CompilerParams(vmem_limit_bytes=24 * MIB),
        name="gather",
    )(arrived.reshape(DEV, TILES, 8, W))
    return (state_after, new_integrals.transpose(1, 0, 2))


def solution(mesh):
    return jax.shard_map(
        on_device,
        mesh=mesh,
        in_specs=(
            P(None, "cut", "depth", None),
            P("cut", "depth", None),
            P("cut", "depth"),
            P("cut", "depth"),
            P(("cut", "depth"), None, None),
            P(("cut", "depth"), None),
            P(("cut", "depth")),
        ),
        out_specs=(P(None, "cut", "depth", None), P(("cut", "depth"), None, None)),
        check_vma=False,
    )
```

```python
import jax
import jax.numpy as jnp
from jax import lax
from jax.experimental import pallas as pl
from jax.experimental.pallas import tpu as pltpu
from jax.sharding import PartitionSpec as P

f32 = jnp.float32
N = 16
R = 4
E = N + 2 * R
W = 128
DEV = 128
CAP = 6
TILES = CAP + 1
SLOTS = 256
BIG = 1e30
MIB = 1024 * 1024

REACH = (4, 3, 3, 4, 3, 4, 3, 3, 3, 3, 2)
STARTS = tuple(sum(REACH[:field]) for field in range(10))
LIMIT_SLAB = sum(REACH[:10])
SLABS = LIMIT_SLAB + 1
WIDTH = (3, 4, 3, 4, 4, 3, 3, 3, 3, 3, 2)
RADIUS = (4,) * 6 + (3,) * 4 + (2,)


def pieces(corners, at):
    found = {}
    for field in range(11):
        for r in range(E):
            beyond = max(R - r, r - (R + N - 1), 0)
            width = WIDTH[field] if beyond == 0 else RADIUS[field] - beyond
            if width > 0 and (beyond > 0) == corners:
                found[field, r] = (width, at)
                at += width
    return found, at


BESIDE, BESIDE_ROWS = pieces(False, 0)
CORNERS, PIECE_ROWS = pieces(True, BESIDE_ROWS)
PIECES = BESIDE | CORNERS
SIDE_ROWS = -(-PIECE_ROWS // 8) * 8
CORNER_ROWS = SIDE_ROWS - BESIDE_ROWS


def is_odd(axis):
    return lax.rem(lax.axis_index(axis), 2) == 1


def limit_row(flags_ref, stress_ref, row):
    along = jnp.where(
        flags_ref[row : row + 1] == 1, stress_ref[row : row + 1], BIG
    )
    square = jnp.broadcast_to(along, (N, N))
    diagonal = lax.broadcasted_iota(jnp.int32, (N, N), 0) == lax.broadcasted_iota(
        jnp.int32, (N, N), 1
    )
    column = jnp.sum(jnp.where(diagonal, square, 0.0), axis=1, keepdims=True)
    return jnp.broadcast_to(column, (N, W))


def scaled_inverse(density):
    return 0.075 / density


def pack_cut(
    flags_hbm, stress_hbm, state_ref, density_ref, one_ref, two_ref, flags_ref, stress_ref, edges, sems
):
    odd = lax.rem(lax.axis_index("cut"), 2)
    tops = ((one_ref, odd), (two_ref, 1 - odd))
    copies = [
        pltpu.make_async_copy(flags_hbm, flags_ref, sems.at[20]),
        pltpu.make_async_copy(stress_hbm, stress_ref, sems.at[21]),
    ]
    for field in range(9):
        source = state_ref.at[3 + field if field < 6 else field - 6]
        reach, start = REACH[field], STARTS[field]
        for side, (target, top) in enumerate(tops):
            copies.append(
                pltpu.make_async_copy(
                    source.at[pl.ds(top * (N - reach), reach)],
                    target.at[pl.ds(start, reach)],
                    sems.at[2 * field + side],
                )
            )
    for side, (target, top) in enumerate(tops):
        copies.append(
            pltpu.make_async_copy(
                density_ref.at[pl.ds(top * (N - 3), 3)], edges.at[side], sems.at[18 + side]
            )
        )
    for copy in copies:
        copy.start()
    copies[0].wait()
    copies[1].wait()
    half = lax.broadcasted_iota(jnp.int32, (N, W), 1) < W // 2
    slabs = [
        jnp.where(
            half,
            limit_row(flags_ref, stress_ref, row),
            limit_row(flags_ref, stress_ref, row + 1),
        )
        for row in (0, N - 2)
    ]
    for target, top in tops:
        target[LIMIT_SLAB] = jnp.where(top == 1, slabs[1], slabs[0])
    for copy in copies[2:]:
        copy.wait()
    for side, (target, top) in enumerate(tops):
        for row in range(3):
            target[STARTS[9] + row] = scaled_inverse(edges[side, row])


def cut_row(field, r, odd, one_ref, two_ref):
    def came(slab):
        one, two = one_ref[slab], two_ref[slab]
        return jnp.where(odd, two, one) if r < R else jnp.where(odd, one, two)

    if field == 10:
        slab = came(LIMIT_SLAB)
        first = lax.broadcasted_iota(jnp.int32, (N, W), 1) < W // 2
        wanted = first if r in (R - 2, R + N) else ~first
        return jnp.where(wanted, slab, pltpu.roll(slab, W // 2, 1))
    return came(STARTS[field] + (r - (R - REACH[field]) if r < R else r - R - N))


def own_row(field, row, flags_ref, yield_ref, state_ref, density_ref):
    if field < 6:
        return state_ref[3 + field, row]
    if field < 9:
        return state_ref[field - 6, row]
    if field == 9:
        return scaled_inverse(density_ref[row])
    return limit_row(flags_ref, yield_ref, row)


def put_piece(row, width, odd, one_ref, one_at, two_ref, two_at):
    low, high = row[:width], row[N - width :]
    one_ref[one_at : one_at + width] = jnp.where(odd, high, low)
    two_ref[two_at : two_at + width] = jnp.where(odd, low, high)


def pack_beside(
    flags_hbm,
    yield_hbm,
    state_hbm,
    density_hbm,
    one_ref,
    two_ref,
    flags_ref,
    yield_ref,
    state_ref,
    density_ref,
    sems,
):
    pairs = (
        (flags_hbm, flags_ref),
        (yield_hbm, yield_ref),
        (state_hbm, state_ref),
        (density_hbm, density_ref),
    )
    copies = [
        pltpu.make_async_copy(source, target, sems.at[k])
        for k, (source, target) in enumerate(pairs)
    ]
    for copy in copies:
        copy.start()
    for copy in copies:
        copy.wait()
    odd = is_odd("depth")
    for (field, r), (width, at) in BESIDE.items():
        row = own_row(field, r - R, flags_ref, yield_ref, state_ref, density_ref)
        put_piece(row, width, odd, one_ref, at, two_ref, at)


def pack_corners(cut_one_ref, cut_two_ref, beside_two_ref, one_ref, two_ref):
    two_ref[:BESIDE_ROWS] = beside_two_ref[...]
    odd_cut, odd = is_odd("cut"), is_odd("depth")
    for (field, r), (width, at) in CORNERS.items():
        row = cut_row(field, r, odd_cut, cut_one_ref, cut_two_ref)
        put_piece(row, width, odd, one_ref, at - BESIDE_ROWS, two_ref, at)


def steps_and_remap(
    place_ref,
    flags_ref,
    yield_ref,
    state_ref,
    density_ref,
    cut_one_ref,
    cut_two_ref,
    beside_one_ref,
    corner_one_ref,
    side_two_ref,
    labels_ref,
    ready_ref,
    weights_ref,
    after_ref,
    outgoing_ref,
    tension,
    velocity,
    inverse,
    limits,
    rows_even,
    rows_odd,
    after,
    held,
    sems,
    after_sem,
):
    per = 2 * N

    def fetch(cx):
        return pltpu.make_async_copy(
            weights_ref.at[pl.ds(cx * per, per)],
            held.at[pl.ds((cx - READY) * per, per)],
            sems.at[cx - READY],
        )

    for cx in range(READY, N):
        fetch(cx).start()

    odd_cut, odd_depth = is_odd("cut"), is_odd("depth")
    for field in range(11):
        reach = REACH[field]
        for r in range(R - reach, R + N + reach):
            if R <= r < R + N:
                own = own_row(field, r - R, flags_ref, yield_ref, state_ref, density_ref)
            else:
                own = cut_row(field, r, odd_cut, cut_one_ref, cut_two_ref)
            width, at = PIECES.get((field, r), (0, 0))
            if width == 0:
                beside = [jnp.zeros((8, W), f32)]
            else:
                two = side_two_ref[at : at + width]
                if at < BESIDE_ROWS:
                    one = beside_one_ref[at : at + width]
                else:
                    one = corner_one_ref[at - BESIDE_ROWS : at - BESIDE_ROWS + width]
                beside = [jnp.where(odd_depth, one, two), jnp.where(odd_depth, two, one)]
                if width < 4:
                    beside.insert(1, jnp.zeros((8 - 2 * width, W), f32))
            if field < 6:
                target = tension.at[field, r]
            elif field < 9:
                target = velocity.at[field - 6, r]
            else:
                target = (inverse if field == 9 else limits).at[r]
            target[:N] = own
            target[N:] = jnp.concatenate(beside, 0)

    def label(i, carry):
        for j in range(8):
            owner = i * 8 + j
            outgoing_ref[owner * TILES + CAP] = jnp.broadcast_to(labels_ref[owner], (8, W))
        return carry

    lax.fori_loop(0, DEV // 8, label, 0)

    lane = lax.broadcasted_iota(jnp.int32, (E, W), 1)
    first, last = lane == 0, lane == W - 1

    def along_depth(x):
        return pltpu.roll(x, E - 1, 0) - pltpu.roll(x, 1, 0)

    def along_width(x):
        up = jnp.where(last, 0.0, pltpu.roll(x, W - 1, 1))
        down = jnp.where(first, 0.0, pltpu.roll(x, 1, 1))
        return up - down

    def new_velocity(r):
        def along_cut(field):
            return tension[field, r + 1] - tension[field, r - 1]

        scale = inverse[r]
        xy, yz, xz = tension[3, r], tension[4, r], tension[5, r]
        return (
            velocity[0, r] + (along_cut(0) + along_depth(xy) + along_width(xz)) * scale,
            velocity[1, r] + (along_cut(3) + along_depth(tension[1, r]) + along_width(yz)) * scale,
            velocity[2, r] + (along_cut(5) + along_depth(yz) + along_width(tension[2, r])) * scale,
        )

    def new_stress(r):
        vx, vy, vz = velocity[0, r], velocity[1, r], velocity[2, r]
        limit = limits[r]

        def along_cut(field):
            return velocity[field, r + 1] - velocity[field, r - 1]

        xx, yy, zz = along_cut(0), along_depth(vy), along_width(vz)
        bulk = 0.075 * (xx + yy + zz)
        sxx = tension[0, r] + (0.09 * xx + bulk)
        syy = tension[1, r] + (0.09 * yy + bulk)
        szz = tension[2, r] + (0.09 * zz + bulk)
        sxy = tension[3, r] + 0.045 * (along_depth(vx) + along_cut(1))
        syz = tension[4, r] + 0.045 * (along_width(vy) + along_depth(vz))
        sxz = tension[5, r] + 0.045 * (along_width(vx) + along_cut(2))
        p = (sxx + syy + szz) * (1.0 / 3.0)
        dxx, dyy, dzz = sxx - p, syy - p, szz - p
        square = 1.5 * (
            dxx * dxx + dyy * dyy + dzz * dzz + 2.0 * (sxy * sxy + syz * syz + sxz * sxz)
        )
        factor = jnp.minimum(1.0, limit * lax.rsqrt(square))
        inside = limit > 0.0
        new = (
            p + factor * dxx,
            p + factor * dyy,
            p + factor * dzz,
            factor * sxy,
            factor * syz,
            factor * sxz,
        )
        return [jnp.where(inside, x, 0.0) for x in new]

    def sweep(start, stop, update, target):
        for low in range(start, stop, GROUP):
            at = range(low, min(low + GROUP, stop))
            for r, result in zip(at, [update(r) for r in at]):
                for field, x in enumerate(result):
                    target[field, r] = x

    def finish(i, target):
        at = range(BATCH * i, BATCH * (i + 1))
        results = [new_stress(cx + R) for cx in at]
        for j, (cx, result) in enumerate(zip(at, results)):
            fields = [velocity[f, cx + R] for f in range(3)] + result
            for field, x in enumerate(fields):
                own = x[:N]
                after[field, cx] = own
                target[j, pl.ds(field, N, stride=16)] = own

    def remap(i, source):
        none = jnp.zeros((16, W), jnp.bfloat16)
        for j in range(BATCH):
            for cy in range(0, N, 2):
                one = source[j, cy * 16 : (cy + 1) * 16].astype(jnp.bfloat16)
                two = source[j, (cy + 1) * 16 : (cy + 2) * 16].astype(jnp.bfloat16)
                blocks = jnp.concatenate(
                    [jnp.concatenate([one, none], 1), jnp.concatenate([none, two], 1)], 0
                )
                pair = (BATCH * i + j) * per + 2 * cy
                here, at = (ready_ref, pair) if BATCH * i < READY else (held, pair - READY * per)
                spread = jnp.concatenate(
                    [
                        jnp.concatenate([here[at], here[at + 1]], 1),
                        jnp.concatenate([here[at + 2], here[at + 3]], 1),
                    ],
                    0,
                )
                result = jnp.dot(blocks, spread, preferred_element_type=f32)
                for k in range(4):
                    place = place_ref[pair + k]
                    base = (place >> 3) * TILES
                    rank = place & 7
                    row, column = 16 * (k // 2), W * (k % 2)
                    part = result[row : row + 9, column : column + W]
                    outgoing_ref[base + rank] = part[:8]
                    outgoing_ref[base + CAP, pl.ds(rank, 1)] = part[8:9]

    keep = pltpu.make_async_copy(after, after_ref, after_sem)
    batches = N // BATCH
    for i in range(batches + 1):
        for cx in range(max(READY, BATCH * (i - 1)), BATCH * i):
            fetch(cx).wait()
        if i < batches:
            end = R + BATCH * (i + 1)
            sweep(end - BATCH + 3 if i else 1, end + 3, new_velocity, velocity)
            sweep(end - BATCH + 2 if i else 2, end + 2, new_stress, tension)
            sweep(end - BATCH + 1 if i else 3, end + 1, new_velocity, velocity)
            finish(i, (rows_even, rows_odd)[i % 2])
        if i == batches - 1:
            keep.start()
        if i > 0:
            remap(i - 1, (rows_even, rows_odd)[(i - 1) % 2])
    keep.wait()


BATCH = 4
READY = 4
GROUP = 4
PARTS = 3
ROOM = SLOTS + 8


def gather(arrived, out_ref, turned, slots, sem, *sums):
    main, rest = sums[:PARTS], sums[PARTS:]
    named = arrived[:, CAP, CAP, :].T[:8].astype(jnp.int32)
    turned[...] = jnp.where(named == 0, SLOTS, named - 1)
    copy = pltpu.make_async_copy(turned, slots, sem)
    copy.start()
    for k in range(PARTS):
        main[k][...] = jnp.zeros((8 * ROOM, W), f32)
        rest[k][...] = jnp.zeros((ROOM, W), f32)
    copy.wait()

    def sources(i, carry):
        for j in range(UNROLL):
            source = i * UNROLL + j
            for k in range(CAP):
                part = k % PARTS
                slot = slots[k, source]
                tile = pl.ds(pl.multiple_of(slot * 8, 8), 8)
                main[part][tile] += arrived[source, k]
                rest[part][pl.ds(slot, 1)] += arrived[source, CAP, k : k + 1]
        return carry

    lax.fori_loop(0, DEV // UNROLL, sources, 0)

    def total(parts, spot):
        return parts[0][spot] + parts[1][spot] + parts[2][spot]

    def fold(i, carry):
        spot = pl.ds(pl.multiple_of(i * W, W), W)
        main[0][spot] = total(main, spot)
        return carry

    lax.fori_loop(0, 8 * SLOTS // W, fold, 0)
    for field in range(8):
        out_ref[field] = main[0][pl.ds(field, SLOTS, stride=8)]
    out_ref[8] = total(rest, pl.ds(0, SLOTS))


UNROLL = 4


def bring(weights_ref, ready_ref, sems):
    part = READY * 2 * N // 8
    copies = [
        pltpu.make_async_copy(
            weights_ref.at[pl.ds(k * part, part)], ready_ref.at[pl.ds(k * part, part)], sems.at[k]
        )
        for k in range(8)
    ]
    for copy in copies:
        copy.start()
    for copy in copies:
        copy.wait()


def exchange(x, axis, first):
    pairs = [(i, i + 1) for i in range(first, lax.axis_size(axis) - 1, 2)]
    return lax.ppermute(x, axis, pairs + [(high, low) for low, high in pairs])


VM = pl.BlockSpec(memory_space=pltpu.VMEM)
SM = pl.BlockSpec(memory_space=pltpu.SMEM)
HB = pl.BlockSpec(memory_space=pltpu.HBM)
SMALL = pltpu.CompilerParams(vmem_limit_bytes=8 * MIB)


def stay(x):
    return pltpu.with_memory_space_constraint(x, pltpu.HBM)


def both(rows):
    return (jax.ShapeDtypeStruct(rows + (W,), f32),) * 2


def on_device(
    initial_state, density, yield_flags, yield_stress, crossing_weights, new_owner, new_slot
):
    given = [stay(x) for x in (yield_flags, yield_stress, initial_state, density)]
    one, two = pl.pallas_call(
        pack_cut,
        out_shape=both((SLABS, N)),
        in_specs=[HB] * 4,
        out_specs=(VM, VM),
        scratch_shapes=[
            pltpu.VMEM((N, N), jnp.int32),
            pltpu.VMEM((N, N), f32),
            pltpu.VMEM((2, 3, N, W), f32),
            pltpu.SemaphoreType.DMA((22,)),
        ],
        compiler_params=SMALL,
        name="pack_cut",
    )(*given)
    cut_one, cut_two = exchange(one, "cut", 1), exchange(two, "cut", 0)
    beside_one, beside_two = pl.pallas_call(
        pack_beside,
        out_shape=both((BESIDE_ROWS,)),
        in_specs=[HB] * 4,
        out_specs=(VM, VM),
        scratch_shapes=[
            pltpu.VMEM((N, N), jnp.int32),
            pltpu.VMEM((N, N), f32),
            pltpu.VMEM((9, N, N, W), f32),
            pltpu.VMEM((N, N, W), f32),
            pltpu.SemaphoreType.DMA((4,)),
        ],
        compiler_params=SMALL,
        name="pack_beside",
    )(*given)
    beside_one, beside_two, weights = lax.optimization_barrier(
        (beside_one, beside_two, crossing_weights)
    )
    beside_one = exchange(beside_one, "depth", 1)
    owners = new_owner[:, 0]
    hits = (owners[:, None] == jnp.arange(DEV, dtype=jnp.int32)[None, :]).astype(jnp.int32)
    rank = jnp.sum((jnp.cumsum(hits, 0) - hits) * hits, 1)
    place = owners * 8 + rank
    by_rank = jnp.where(
        rank[:, None] == jnp.arange(W, dtype=jnp.int32)[None, :], new_slot[:, None] + 1, 0
    )
    labels = lax.dot_general(
        hits.astype(jnp.bfloat16),
        by_rank.astype(jnp.bfloat16),
        (((0,), (0,)), ((), ())),
        preferred_element_type=f32,
    )
    cut_one, cut_two, labels, place = lax.optimization_barrier((cut_one, cut_two, labels, place))
    one, two = pl.pallas_call(
        pack_corners,
        out_shape=both((CORNER_ROWS,))[:1] + both((SIDE_ROWS,))[:1],
        in_specs=[VM] * 3,
        out_specs=(VM, VM),
        compiler_params=SMALL,
        name="pack_corners",
    )(cut_one, cut_two, beside_two)
    corner_one, side_two = exchange(one, "depth", 1), exchange(two, "depth", 0)
    ready = pl.pallas_call(
        bring,
        out_shape=jax.ShapeDtypeStruct((READY * 2 * N, W, W), jnp.bfloat16),
        in_specs=[HB],
        out_specs=VM,
        scratch_shapes=[pltpu.SemaphoreType.DMA((8,))],
        compiler_params=pltpu.CompilerParams(vmem_limit_bytes=12 * MIB),
        cost_estimate=pl.CostEstimate(
            flops=0, bytes_accessed=READY * 2 * N * W * W * 2, transcendentals=0
        ),
        name="bring",
    )(stay(weights))

    state_after, outgoing = pl.pallas_call(
        steps_and_remap,
        out_shape=(
            jax.ShapeDtypeStruct((9, N, N, W), f32),
            jax.ShapeDtypeStruct((DEV * TILES, 8, W), f32),
        ),
        in_specs=[SM] + [VM] * 11 + [HB],
        out_specs=(HB, VM),
        scratch_shapes=[
            pltpu.VMEM((6, E, E, W), f32),
            pltpu.VMEM((3, E, E, W), f32),
            pltpu.VMEM((E, E, W), f32),
            pltpu.VMEM((E, E, W), f32),
            pltpu.VMEM((BATCH, N * 16, W), f32),
            pltpu.VMEM((BATCH, N * 16, W), f32),
            pltpu.VMEM((9, N, N, W), f32),
            pltpu.VMEM(((N - READY) * 2 * N, W, W), jnp.bfloat16),
            pltpu.SemaphoreType.DMA((N - READY,)),
            pltpu.SemaphoreType.DMA,
        ],
        compiler_params=pltpu.CompilerParams(vmem_limit_bytes=24 * MIB),
        name="steps_and_remap",
    )(
        place,
        yield_flags,
        yield_stress,
        initial_state,
        density,
        cut_one,
        cut_two,
        beside_one,
        corner_one,
        side_two,
        labels[:, None, :],
        ready,
        stay(crossing_weights),
    )
    arrived = lax.all_to_all(outgoing, ("cut", "depth"), split_axis=0, concat_axis=0, tiled=True)
    new_integrals = pl.pallas_call(
        gather,
        out_shape=jax.ShapeDtypeStruct((9, SLOTS, W), f32),
        in_specs=[VM],
        out_specs=VM,
        scratch_shapes=[
            pltpu.VMEM((8, W), jnp.int32),
            pltpu.SMEM((8, W), jnp.int32),
            pltpu.SemaphoreType.DMA,
        ]
        + [pltpu.VMEM((8 * ROOM, W), f32)] * PARTS
        + [pltpu.VMEM((ROOM, W), f32)] * PARTS,
        compiler_params=pltpu.CompilerParams(vmem_limit_bytes=24 * MIB),
        name="gather",
    )(arrived.reshape(DEV, TILES, 8, W))
    return (state_after, new_integrals.transpose(1, 0, 2))


def solution(mesh):
    return jax.shard_map(
        on_device,
        mesh=mesh,
        in_specs=(
            P(None, "cut", "depth", None),
            P("cut", "depth", None),
            P("cut", "depth"),
            P("cut", "depth"),
            P(("cut", "depth"), None, None),
            P(("cut", "depth"), None),
            P(("cut", "depth")),
        ),
        out_specs=(P(None, "cut", "depth", None), P(("cut", "depth"), None, None)),
        check_vma=False,
    )
```
